32 devices in a mesh: row: 8 (over z, x), col: 4 (over y, core).
Axes of the slice: x: 2, y: 2, z: 4, core: 2. Of those that a mesh axis runs over, the one named last changes fastest.
Arguments:
- features: bfloat16 [4096, 128], P(('row', 'col')), may hold values from -6 to 6
- cotangent: bfloat16 [4096, 128], P(('row', 'col')), may hold values from -6 to 6
- self_weight: bfloat16 [128, 128], replicated, may hold values from -0.5 to 0.5
- neigh_weight: bfloat16 [128, 128], replicated, may hold values from -0.5 to 0.5
- degrees: int32 [4096], P(('row', 'col')), may hold values from 512 to 2048
- adjacency: int32 [8, 4, 64, 128, 128], P('row', 'col'), may hold values 0 or 1
- tile_rows: int32 [8, 4, 64], P('row', 'col'), may hold values from 0 to 7
- tile_cols: int32 [8, 4, 64], P('row', 'col'), may hold values from 0 to 3
- tile_count: int32 [8, 4], P('row', 'col'), may hold values from 32 to 64, as said below
Outputs:
- hidden: bfloat16 [4096, 128], P(('row', 'col'))
- grad_features: bfloat16 [4096, 128], P(('row', 'col'))
- grad_self: float32 [128, 128], replicated
- grad_neigh: float32 [128, 128], replicated
The draws below stay inside these ranges and needn't reach their ends.
Inputs may be any that keep to these rules, and one draw needn't show every extreme that they name: `tile_count`: each device has between 64 // 2 (at least 1) and 64 live slots; in every draw some device has exactly 64. `tile_rows`: only a device's first tile_count slots are live; places may repeat. `tile_cols`: only a device's first tile_count slots are live; places may repeat.
All inputs are finite; a program needn't handle non-finite values. No bound on the sum of `adjacency` on one device may be relied on, other than what follows from the above.
Results may differ from the reference program's by a relative error of at most 0.024.
Values may be sent and summed in bfloat16 or wider, within the bound.
A program may use at most 64 MiB of HBM per device.

```python
import jax
import jax.numpy as jnp
from jax import lax

F = 128
BLK = 128
BPD = 1
K = 64
ROWB = 8
COLB = 4
NODES = 4096
N_ROW = 8
N_COL = 4


def draw_tile_count(key, part):
    key = jax.random.fold_in(key, 7)
    first_key, second_key = jax.random.split(key)
    counts = jax.random.randint(first_key, (N_ROW * N_COL,), max(1, K // 2), K + 1, dtype=jnp.int32)
    chosen = jax.random.randint(second_key, (), 0, N_ROW * N_COL, dtype=jnp.int32)
    positions = jnp.arange(N_ROW * N_COL, dtype=jnp.int32)
    counts = jnp.where(positions == chosen, K, counts).astype(jnp.int32)
    return counts.reshape(N_ROW, N_COL)


def set_ends(array, key, low, top_value):
    longest = array.shape.index(max(array.shape))
    spots = []
    for shift in (0, 1):
        where = [jax.random.randint(jax.random.fold_in(key, axis), (), 0, length) for axis, length in enumerate(array.shape)]
        where[longest] = (where[longest] + shift) % array.shape[longest]
        spots.append(tuple(where))
    return array.at[spots[0]].set(low).at[spots[1]].set(top_value)


def steps_of(key, dims, cuts, low, largest):
    loudness = 1.0
    for axis_at, parts in cuts:
        steps = jax.random.uniform(jax.random.fold_in(jax.random.fold_in(key, 6), axis_at), (parts,), jnp.float32, low / len(cuts), largest / len(cuts))
        loudness = loudness * jnp.repeat(jnp.exp(steps), dims[axis_at] // parts).reshape((-1,) + (1,) * (len(dims) - 1 - axis_at))
    return loudness


def noise(rng, dims, scale, bound, cuts=(), held_as=jnp.bfloat16):
    array = jax.random.normal(rng, dims, jnp.float32) * scale
    if len(cuts) > 0:
        array = steps_of(rng, dims, cuts, -0.22, 0.18) * array
    return jnp.clip(array, min=-bound, max=bound).astype(held_as)


def setup_inputs(seed: int = 0) -> dict:
    key_of = jax.random.split(jax.random.key(seed), 10)
    return {
        "features": noise(key_of[0], (NODES, F), 1.0, 6.0, ((0, 32),)),
        "cotangent": noise(key_of[1], (NODES, F), 1.0, 6.0, ((0, 32),)),
        "self_weight": noise(key_of[2], (F, F), F ** -0.5, 0.5),
        "neigh_weight": noise(key_of[3], (F, F), F ** -0.5, 0.5),
        "degrees": set_ends(jax.random.randint(key_of[4], (NODES,), max(1, K * BLK // (16 * BPD)), K * BLK // (4 * BPD) + 1), jax.random.fold_in(key_of[4], 1), max(1, K * BLK // (16 * BPD)), (K * BLK // (4 * BPD) + 1) - 1).astype(jnp.int32),
        "adjacency": set_ends((jax.random.randint(key_of[5], (N_ROW, N_COL, K, BLK, BLK), 0, 8) < 1).astype(jnp.int32), jax.random.fold_in(key_of[5], 1), 0, 1),
        "tile_rows": set_ends(jax.random.randint(key_of[6], (N_ROW, N_COL, K), 0, ROWB), jax.random.fold_in(key_of[6], 1), 0, ROWB - 1).astype(jnp.int32),
        "tile_cols": set_ends(jax.random.randint(key_of[7], (N_ROW, N_COL, K), 0, COLB), jax.random.fold_in(key_of[7], 1), 0, COLB - 1).astype(jnp.int32),
        "tile_count": draw_tile_count(jax.random.fold_in(key_of[9], 71), 0),
    }


def tile_sums(tile_bits, pick_blocks, place_blocks, is_live, source, out_blocks, transpose):
    edge = tile_bits.shape[-1]
    source_blocks = source.reshape(-1, edge, source.shape[-1]).astype(jnp.float32)
    chosen = jnp.take(source_blocks, pick_blocks, axis=0)
    bits = tile_bits.astype(jnp.float32)
    if transpose:
        products = jnp.einsum('kji,kjf->kif', bits, chosen, precision=lax.Precision.HIGHEST)
    else:
        products = jnp.einsum('kij,kjf->kif', bits, chosen, precision=lax.Precision.HIGHEST)
    targets = jnp.arange(out_blocks, dtype=jnp.int32)
    select = jnp.where((place_blocks[None, :] == targets[:, None]) & is_live[None, :], 1.0, 0.0).astype(jnp.float32)
    summed = jnp.einsum('bk,kif->bif', select, products, precision=lax.Precision.HIGHEST)
    return summed

def rounded(values):
    return lax.optimization_barrier(values.astype(jnp.bfloat16)).astype(jnp.float32)

def silu_pair(linear):
    sigma = jax.nn.sigmoid(linear)
    return (linear * sigma, sigma * (1.0 + linear * (1.0 - sigma)))

def reference(features, cotangent, self_weight, neigh_weight, degrees, adjacency, tile_rows, tile_cols, tile_count):
    device_count = N_ROW * N_COL
    tile_all = adjacency.reshape(device_count, K, BLK, BLK)
    rows_all = tile_rows.reshape(device_count, K)
    cols_all = tile_cols.reshape(device_count, K)
    count_all = tile_count.reshape(device_count)
    ranks = jnp.arange(device_count, dtype=jnp.int32)
    local_rows = jnp.arange(ROWB, dtype=jnp.int32)
    local_cols = jnp.arange(COLB, dtype=jnp.int32)
    slot_index = jnp.arange(K, dtype=jnp.int32)

    def row_owner(column):
        return ((local_rows // BPD * N_COL + column) * BPD + local_rows % BPD).astype(jnp.int32)

    def forward_step(carry, entry):
        tile_bits, row_ids, col_ids, count, rank = entry
        grid_row = rank // N_COL
        grid_col = rank % N_COL
        is_live = slot_index < count
        summed = tile_sums(tile_bits, grid_row * COLB + col_ids, row_ids, is_live, features, ROWB, False)
        return (carry.at[row_owner(grid_col)].add(rounded(summed)), None)
    start = jnp.zeros((NODES // BLK, BLK, F), jnp.float32)
    gathered, _ = lax.scan(forward_step, start, (tile_all, rows_all, cols_all, count_all, ranks))
    inverse = lax.rsqrt(jnp.maximum(degrees, 1).astype(jnp.float32))[:, None]
    mixed = (gathered.reshape(NODES, F) * inverse).astype(jnp.bfloat16)
    linear = jnp.dot(features, self_weight, preferred_element_type=jnp.float32) + jnp.dot(mixed, neigh_weight, preferred_element_type=jnp.float32)
    activated, slope = silu_pair(linear)
    hidden = activated.astype(jnp.bfloat16)
    grad_linear = (cotangent.astype(jnp.float32) * slope).astype(jnp.bfloat16)
    grad_mixed = (jnp.dot(grad_linear, neigh_weight.T, preferred_element_type=jnp.float32) * inverse).astype(jnp.bfloat16)

    def backward_step(carry, entry):
        tile_bits, row_ids, col_ids, count, rank = entry
        grid_row = rank // N_COL
        grid_col = rank % N_COL
        is_live = slot_index < count
        summed = tile_sums(tile_bits, row_owner(grid_col)[row_ids], col_ids, is_live, grad_mixed, COLB, True)
        return (carry.at[grid_row * COLB + local_cols].add(rounded(summed)), None)
    returned, _ = lax.scan(backward_step, start, (tile_all, rows_all, cols_all, count_all, ranks))
    grad_features = (jnp.dot(grad_linear, self_weight.T, preferred_element_type=jnp.float32) + returned.reshape(NODES, F)).astype(jnp.bfloat16)
    grad_self = jnp.einsum('nf,ng->fg', features.astype(jnp.float32), grad_linear.astype(jnp.float32), precision=lax.Precision.HIGHEST)
    grad_neigh = jnp.einsum('nf,ng->fg', mixed.astype(jnp.float32), grad_linear.astype(jnp.float32), precision=lax.Precision.HIGHEST)
    return (hidden, grad_features, grad_self, grad_neigh)
```

```python
import functools

import jax
import jax.numpy as jnp
from jax import lax
from jax.experimental import pallas as pl
from jax.experimental.pallas import tpu as pltpu
from jax.sharding import PartitionSpec as P

MESH = pl.DeviceIdType.MESH
BF16 = jnp.bfloat16
F32 = jnp.float32
CHUNK = 8


def dot(a, b, contract=((1,), (0,))):
    return lax.dot_general(a, b, (contract, ((), ())), preferred_element_type=F32)


def each(low, high, step):
    if high - low <= 8:
        for index in range(low, high):
            step(index)
    else:
        def looped(index, carry):
            step(index)
            return carry
        lax.fori_loop(low, high, looped, 0)


def place_kernel(chunks, count_ref, rows_ref, cols_ref, tiles_hbm, dense_ref, tiles, sems):
    edge = tiles.shape[-1]
    copies = []
    for index in range(chunks):
        piece = pl.ds(index * CHUNK, CHUNK)
        copy = pltpu.make_async_copy(tiles_hbm.at[piece], tiles.at[piece], sems.at[index])
        copy.start()
        copies.append(copy)
    count = count_ref[0, 0]
    dense_ref[...] = jnp.zeros_like(dense_ref)
    for index in range(chunks):
        copies[index].wait()

        def place(slot, carry):
            row = pl.multiple_of(rows_ref[0, slot] * edge, edge)
            col = pl.multiple_of(cols_ref[0, slot] * edge, edge)
            spot = (pl.ds(row, edge), pl.ds(col, edge))
            dense_ref[spot] = dense_ref[spot] + tiles[slot].astype(F32).astype(BF16)
            return carry

        first = index * CHUNK
        last = jnp.clip(count, first, first + CHUNK)
        lax.fori_loop(first, last, place, 0)


def layer_kernel(
    n_row, n_col,
    feat_ref, cot_ref, self_ref, neigh_ref, deg_ref, dense_hbm,
    hidden_ref, gfeat_ref, gself_ref, gneigh_ref,
    dense, src, part_out, part_in, gm, back_out, back_in, w_out, w_in, q_out, q_in, fin, back_acc,
    dense_sem, src_s, src_r, part_s, part_r, gm_s, gm_r, back_s, back_r,
    w_s, w_r, q_s, q_r, fin_s, fin_r,
):
    r = lax.axis_index("row")
    c = lax.axis_index("col")
    edge = feat_ref.shape[0]

    def row_at(d):
        return lax.rem(r + d, n_row)

    def col_at(d):
        return lax.rem(c + d, n_col)

    def over_row(source, target, send, recv, d):
        return pltpu.make_async_remote_copy(
            src_ref=source, dst_ref=target, send_sem=send.at[d], recv_sem=recv.at[d],
            device_id=(row_at(d), c), device_id_type=MESH)

    def over_col(source, target, send, recv, d):
        return pltpu.make_async_remote_copy(
            src_ref=source, dst_ref=target, send_sem=send.at[d], recv_sem=recv.at[d],
            device_id=(r, col_at(d)), device_id_type=MESH)

    fetch = pltpu.make_async_copy(dense_hbm, dense, dense_sem)
    fetch.start()
    barrier = pltpu.get_barrier_semaphore()
    each(1, n_col, lambda d: pl.semaphore_signal(
        barrier, inc=1, device_id=(r, col_at(d)), device_id_type=MESH))
    each(1, n_row, lambda d: pl.semaphore_signal(
        barrier, inc=1, device_id=(row_at(d), c), device_id_type=MESH))
    pl.semaphore_wait(barrier, n_row + n_col - 2)

    def src_copy(d):
        return over_col(feat_ref, src.at[c], src_s, src_r, d)

    each(1, n_col, lambda d: src_copy(d).start())
    keep = pltpu.make_async_copy(feat_ref, src.at[c], src_r.at[0])
    keep.start()
    inv_row = lax.rsqrt(jnp.maximum(deg_ref[...], 1).astype(F32))
    down = lax.broadcasted_iota(jnp.int32, (edge, edge), 0)
    across = lax.broadcasted_iota(jnp.int32, (edge, edge), 1)
    inv_col = jnp.sum(jnp.where(down == across, inv_row, 0.0), axis=1, keepdims=True)
    own_linear = dot(feat_ref[...], self_ref[...])
    fetch.wait()
    keep.wait()
    each(1, n_col, lambda d: src_copy(d).wait_recv())
    source = src[...].reshape(n_col * edge, src.shape[-1])

    def part_copy(d):
        return over_row(part_out.at[d], part_in.at[d], part_s, part_r, d)

    def partial(d):
        rows = pl.ds(pl.multiple_of(row_at(d) * edge, edge), edge)
        return dot(dense[rows, :], source)

    def send_part(d):
        part_out[d] = partial(d).astype(BF16)
        part_copy(d).start()

    each(1, n_row, send_part)
    agg = partial(0).astype(BF16).astype(F32)
    for d in range(1, n_row):
        part_copy(d).wait_recv()
        agg = agg + part_in[d].astype(F32)

    mixed = (agg * inv_col).astype(BF16)
    linear = own_linear + dot(mixed, neigh_ref[...])
    sigma = jax.nn.sigmoid(linear)
    slope = sigma * (1.0 + linear * (1.0 - sigma))
    grad_linear = (cot_ref[...].astype(F32) * slope).astype(BF16)
    gm[r] = (dot(neigh_ref[...], grad_linear, ((1,), (1,))) * inv_row).astype(BF16)

    def gm_copy(d):
        return over_row(gm.at[r], gm.at[r], gm_s, gm_r, d)

    each(1, n_row, lambda d: gm_copy(d).start())

    share = w_out.shape[1]
    both = jnp.concatenate([feat_ref[...], mixed], axis=1)
    w_out[...] = dot(both, grad_linear, ((0,), (0,))).reshape(w_out.shape)

    def w_copy(d):
        return over_col(w_out.at[col_at(d)], w_in.at[d], w_s, w_r, d)

    each(1, n_col, lambda d: w_copy(d).start())
    hidden_ref[...] = (linear * sigma).astype(BF16)
    own_grad = dot(grad_linear, self_ref[...], ((1,), (1,)))

    def q_copy(d):
        return over_row(q_out, q_in.at[d], q_s, q_r, d)

    def sum_over_col():
        total = w_out[c]
        for d in range(1, n_col):
            w_copy(d).wait_recv()
            total = total + w_in[d]
        q_out[...] = total.astype(BF16)
        each(1, n_row, lambda d: q_copy(d).start())
        return total

    def back_term(d):
        owner = lax.rem(r - d + n_row, n_row)
        rows = pl.ds(pl.multiple_of(owner * edge, edge), edge)
        return dot(gm[owner], dense[rows, :])

    def add_back(d):
        gm_copy(d).wait_recv()
        back_acc[...] += back_term(d)

    middle = (n_row + 1) // 2
    back_acc[...] = back_term(0)
    each(1, middle, add_back)
    total = sum_over_col()
    each(middle, n_row, add_back)

    for b in range(n_col):
        back_out[b] = back_acc[:, b * edge:(b + 1) * edge].astype(BF16)

    def back_copy(d):
        return over_col(back_out.at[col_at(d)], back_in.at[d], back_s, back_r, d)

    each(1, n_col, lambda d: back_copy(d).start())

    for d in range(1, n_row):
        q_copy(d).wait_recv()
        total = total + q_in[d].astype(F32)
    fin[c] = total.astype(BF16)

    def fin_copy(d):
        return over_col(fin.at[c], fin.at[c], fin_s, fin_r, d)

    each(1, n_col, lambda d: fin_copy(d).start())

    returned = back_out[c].astype(F32)
    for d in range(1, n_col):
        back_copy(d).wait_recv()
        returned = returned + back_in[d].astype(F32)
    gfeat_ref[...] = (own_grad + returned.T).astype(BF16)

    each(1, n_col, lambda d: fin_copy(d).wait_recv())
    grads = fin[...].reshape(n_col * share, fin.shape[-1]).astype(F32)
    half = gself_ref.shape[0]
    gself_ref[...] = grads[:half]
    gneigh_ref[...] = grads[half:]

    def drain_col(d):
        for copy in (src_copy, w_copy, back_copy, fin_copy):
            copy(d).wait_send()

    def drain_row(d):
        for copy in (part_copy, gm_copy, q_copy):
            copy(d).wait_send()

    each(1, n_col, drain_col)
    each(1, n_row, drain_row)


def body(n_row, n_col, features, cotangent, self_weight, neigh_weight, degrees,
         adjacency, tile_rows, tile_cols, tile_count):
    edge = adjacency.shape[-1]
    capacity = adjacency.shape[2]
    hidden_units = features.shape[-1]
    chunks = capacity // CHUNK
    rows, cols = n_row * edge, n_col * edge
    smem = pl.BlockSpec(memory_space=pltpu.SMEM)
    vmem = pl.BlockSpec(memory_space=pltpu.VMEM)
    anywhere = pl.BlockSpec(memory_space=pl.ANY)
    dense = pl.pallas_call(
        functools.partial(place_kernel, chunks),
        out_shape=jax.ShapeDtypeStruct((rows, cols), BF16),
        in_specs=[smem, smem, smem, anywhere],
        out_specs=vmem,
        scratch_shapes=[
            pltpu.VMEM((capacity, edge, edge), jnp.int32),
            pltpu.SemaphoreType.DMA((chunks,)),
        ],
        compiler_params=pltpu.CompilerParams(vmem_limit_bytes=60 * 2**20),
        name="place_tiles",
    )(
        tile_count.reshape(1, 1),
        tile_rows.reshape(1, capacity),
        tile_cols.reshape(1, capacity),
        adjacency.reshape(capacity, edge, edge),
    )
    share = 2 * hidden_units // n_col
    block = (edge, hidden_units)
    dma = pltpu.SemaphoreType.DMA
    return pl.pallas_call(
        functools.partial(layer_kernel, n_row, n_col),
        out_shape=(
            jax.ShapeDtypeStruct(block, BF16),
            jax.ShapeDtypeStruct(block, BF16),
            jax.ShapeDtypeStruct(self_weight.shape, F32),
            jax.ShapeDtypeStruct(neigh_weight.shape, F32),
        ),
        in_specs=[vmem] * 5 + [anywhere],
        out_specs=(vmem,) * 4,
        scratch_shapes=[
            pltpu.VMEM((rows, cols), BF16),
            pltpu.VMEM((n_col,) + block, BF16),
            pltpu.VMEM((n_row,) + block, BF16),
            pltpu.VMEM((n_row,) + block, BF16),
            pltpu.VMEM((n_row,) + block, BF16),
            pltpu.VMEM((n_col,) + block, BF16),
            pltpu.VMEM((n_col,) + block, BF16),
            pltpu.VMEM((n_col, share, hidden_units), F32),
            pltpu.VMEM((n_col, share, hidden_units), F32),
            pltpu.VMEM((share, hidden_units), BF16),
            pltpu.VMEM((n_row, share, hidden_units), BF16),
            pltpu.VMEM((n_col, share, hidden_units), BF16),
            pltpu.VMEM((hidden_units, cols), F32),
            dma,
            dma((n_col,)), dma((n_col,)),
            dma((n_row,)), dma((n_row,)),
            dma((n_row,)), dma((n_row,)),
            dma((n_col,)), dma((n_col,)),
            dma((n_col,)), dma((n_col,)),
            dma((n_row,)), dma((n_row,)),
            dma((n_col,)), dma((n_col,)),
        ],
        compiler_params=pltpu.CompilerParams(
            collective_id=0, has_side_effects=True, vmem_limit_bytes=48 * 2**20),
        name="layer_exchange",
    )(features, cotangent, self_weight, neigh_weight, degrees.reshape(1, edge), dense)


def solution(mesh):
    in_specs = (
        P(("row", "col"), None),
        P(("row", "col"), None),
        P(),
        P(),
        P(("row", "col")),
        P("row", "col", None, None, None),
        P("row", "col", None),
        P("row", "col", None),
        P("row", "col"),
    )
    out_specs = (P(("row", "col"), None), P(("row", "col"), None), P(), P())
    n_row, n_col = mesh.shape["row"], mesh.shape["col"]
    return jax.shard_map(functools.partial(body, n_row, n_col), mesh=mesh,
                         in_specs=in_specs, out_specs=out_specs, check_vma=False)
```

```python
import functools

import jax
import jax.numpy as jnp
from jax import lax
from jax.experimental import pallas as pl
from jax.experimental.pallas import tpu as pltpu
from jax.sharding import PartitionSpec as P

MESH = pl.DeviceIdType.MESH
BF16 = jnp.bfloat16
F32 = jnp.float32
CHUNK = 8


def dot(a, b, contract=((1,), (0,))):
    return lax.dot_general(a, b, (contract, ((), ())), preferred_element_type=F32)


def each(low, high, step):
    if high - low <= 8:
        for index in range(low, high):
            step(index)
    else:
        def looped(index, carry):
            step(index)
            return carry
        lax.fori_loop(low, high, looped, 0)


def place_kernel(chunks, count_ref, rows_ref, cols_ref, tiles_hbm, dense_ref, tiles, sems):
    edge = tiles.shape[-1]
    copies = []
    for index in range(chunks):
        piece = pl.ds(index * CHUNK, CHUNK)
        copy = pltpu.make_async_copy(tiles_hbm.at[piece], tiles.at[piece], sems.at[index])
        copy.start()
        copies.append(copy)
    count = count_ref[0, 0]
    dense_ref[...] = jnp.zeros_like(dense_ref)
    for index in range(chunks):
        copies[index].wait()
        for slot in range(index * CHUNK, (index + 1) * CHUNK):
            live = slot < count
            row = pl.multiple_of(jnp.where(live, rows_ref[0, slot], 0) * edge, edge)
            col = pl.multiple_of(jnp.where(live, cols_ref[0, slot], 0) * edge, edge)
            spot = (pl.ds(row, edge), pl.ds(col, edge))
            tile = tiles[slot] * live.astype(jnp.int32)
            dense_ref[spot] = dense_ref[spot] + tile.astype(F32).astype(BF16)


def finish_kernel(*refs):
    count = len(refs) // 2
    sems = refs[-1]
    copies = [pltpu.make_async_copy(refs[i], refs[count + i], sems.at[i]) for i in range(count)]
    for copy in copies:
        copy.start()
    for copy in copies:
        copy.wait()


def layer_kernel(
    n_row, n_col,
    feat_ref, cot_ref, self_ref, neigh_ref, deg_ref, dense,
    hidden_ref, gfeat_ref, gself_ref, gneigh_ref,
    src, part_out, part_in, gm, back_out, back_in, w_out, w_in, q_out, q_in, p_all, fin, back_acc,
    src_s, src_r, part_s, part_r, gm_s, gm_r, back_s, back_r,
    w_s, w_r, q_s, q_r, p_s, p_r, fin_s, fin_r,
):
    r = lax.axis_index("row")
    c = lax.axis_index("col")
    edge = feat_ref.shape[0]

    def row_at(d):
        return lax.rem(r + d, n_row)

    def col_at(d):
        return lax.rem(c + d, n_col)

    def over_row(source, target, send, recv, d):
        return pltpu.make_async_remote_copy(
            src_ref=source, dst_ref=target, send_sem=send.at[d], recv_sem=recv.at[d],
            device_id=(row_at(d), c), device_id_type=MESH)

    def over_col(source, target, send, recv, d):
        return pltpu.make_async_remote_copy(
            src_ref=source, dst_ref=target, send_sem=send.at[d], recv_sem=recv.at[d],
            device_id=(r, col_at(d)), device_id_type=MESH)

    barrier = pltpu.get_barrier_semaphore()
    each(1, n_col, lambda d: pl.semaphore_signal(
        barrier, inc=1, device_id=(r, col_at(d)), device_id_type=MESH))
    each(1, n_row, lambda d: pl.semaphore_signal(
        barrier, inc=1, device_id=(row_at(d), c), device_id_type=MESH))
    pl.semaphore_wait(barrier, n_row + n_col - 2)

    def src_copy(d):
        return over_col(feat_ref, src.at[c], src_s, src_r, d)

    each(1, n_col, lambda d: src_copy(d).start())
    keep = pltpu.make_async_copy(feat_ref, src.at[c], src_r.at[0])
    keep.start()
    inv_row = lax.rsqrt(jnp.maximum(deg_ref[...], 1).astype(F32))
    down = lax.broadcasted_iota(jnp.int32, (edge, edge), 0)
    across = lax.broadcasted_iota(jnp.int32, (edge, edge), 1)
    inv_col = jnp.sum(jnp.where(down == across, inv_row, 0.0), axis=1, keepdims=True)
    own_linear = dot(feat_ref[...], self_ref[...])
    keep.wait()
    each(1, n_col, lambda d: src_copy(d).wait_recv())
    source = src[...].reshape(n_col * edge, src.shape[-1])

    def part_copy(d):
        return over_row(part_out.at[d], part_in.at[d], part_s, part_r, d)

    def partial(d):
        rows = pl.ds(pl.multiple_of(row_at(d) * edge, edge), edge)
        return dot(dense[rows, :], source)

    def send_part(d):
        part_out[d] = partial(d).astype(BF16)
        part_copy(d).start()

    each(1, n_row, send_part)
    agg = partial(0).astype(BF16).astype(F32)
    for d in range(1, n_row):
        part_copy(d).wait_recv()
        agg = agg + part_in[d].astype(F32)

    mixed = (agg * inv_col).astype(BF16)
    linear = own_linear + dot(mixed, neigh_ref[...])
    sigma = jax.nn.sigmoid(linear)
    slope = sigma * (1.0 + linear * (1.0 - sigma))
    grad_linear = (cot_ref[...].astype(F32) * slope).astype(BF16)
    gm[r] = (dot(neigh_ref[...], grad_linear, ((1,), (1,))) * inv_row).astype(BF16)

    def gm_copy(d):
        return over_row(gm.at[r], gm.at[r], gm_s, gm_r, d)

    each(1, n_row, lambda d: gm_copy(d).start())

    share = w_out.shape[1]
    used = share // q_out.shape[1]
    both = jnp.concatenate([feat_ref[...], mixed], axis=1)
    w_out[...] = dot(both, grad_linear, ((0,), (0,))).reshape(w_out.shape)

    def w_copy(d):
        return over_col(w_out.at[col_at(d)], w_in.at[d], w_s, w_r, d)

    each(1, n_col, lambda d: w_copy(d).start())
    hidden_ref[...] = (linear * sigma).astype(BF16)
    own_grad = dot(grad_linear, self_ref[...], ((1,), (1,)))

    def q_copy(d):
        return over_row(q_out.at[row_at(d)], q_in.at[d], q_s, q_r, d)

    def p_copy(d):
        return over_row(p_all.at[r], p_all.at[r], p_s, p_r, d)

    def sum_over_col():
        total = w_out[c]
        for d in range(1, n_col):
            w_copy(d).wait_recv()
            total = total + w_in[d]
        q_out[:used] = total.reshape((used,) + q_out.shape[1:])
        if used < n_row:
            q_out[used:] = jnp.zeros_like(q_out[used:])
        each(1, n_row, lambda d: q_copy(d).start())

    def back_term(d):
        owner = lax.rem(r - d + n_row, n_row)
        rows = pl.ds(pl.multiple_of(owner * edge, edge), edge)
        return dot(gm[owner], dense[rows, :])

    def add_back(d):
        gm_copy(d).wait_recv()
        back_acc[...] += back_term(d)

    middle = (n_row + 1) // 2
    back_acc[...] = back_term(0)
    each(1, middle, add_back)
    sum_over_col()
    each(middle, n_row, add_back)

    for b in range(n_col):
        back_out[b] = back_acc[:, b * edge:(b + 1) * edge].astype(BF16)

    def back_copy(d):
        return over_col(back_out.at[col_at(d)], back_in.at[d], back_s, back_r, d)

    each(1, n_col, lambda d: back_copy(d).start())

    piece = q_out[r]
    for d in range(1, n_row):
        q_copy(d).wait_recv()
        piece = piece + q_in[d]
    p_all[r] = piece
    each(1, n_row, lambda d: p_copy(d).start())

    returned = back_out[c].astype(F32)
    for d in range(1, n_col):
        back_copy(d).wait_recv()
        returned = returned + back_in[d].astype(F32)
    gfeat_ref[...] = (own_grad + returned.T).astype(BF16)

    each(1, n_row, lambda d: p_copy(d).wait_recv())
    fin[c] = p_all[:used].reshape(share, fin.shape[-1]).astype(BF16)

    def fin_copy(d):
        return over_col(fin.at[c], fin.at[c], fin_s, fin_r, d)

    each(1, n_col, lambda d: fin_copy(d).start())
    each(1, n_col, lambda d: fin_copy(d).wait_recv())
    grads = fin[...].reshape(n_col * share, fin.shape[-1]).astype(F32)
    half = gself_ref.shape[0]
    gself_ref[...] = grads[:half]
    gneigh_ref[...] = grads[half:]

    def drain_col(d):
        for copy in (src_copy, w_copy, back_copy, fin_copy):
            copy(d).wait_send()

    def drain_row(d):
        for copy in (part_copy, gm_copy, q_copy, p_copy):
            copy(d).wait_send()

    each(1, n_col, drain_col)
    each(1, n_row, drain_row)


def body(n_row, n_col, features, cotangent, self_weight, neigh_weight, degrees,
         adjacency, tile_rows, tile_cols, tile_count):
    edge = adjacency.shape[-1]
    capacity = adjacency.shape[2]
    hidden_units = features.shape[-1]
    chunks = capacity // CHUNK
    rows, cols = n_row * edge, n_col * edge
    smem = pl.BlockSpec(memory_space=pltpu.SMEM)
    vmem = pl.BlockSpec(memory_space=pltpu.VMEM)
    hbm = pl.BlockSpec(memory_space=pltpu.HBM)
    dense = pl.pallas_call(
        functools.partial(place_kernel, chunks),
        out_shape=jax.ShapeDtypeStruct((rows, cols), BF16),
        in_specs=[smem, smem, smem, hbm],
        out_specs=vmem,
        scratch_shapes=[
            pltpu.VMEM((capacity, edge, edge), jnp.int32),
            pltpu.SemaphoreType.DMA((chunks,)),
        ],
        compiler_params=pltpu.CompilerParams(vmem_limit_bytes=51 * 2**20),
        name="place_tiles",
    )(
        tile_count.reshape(1, 1),
        tile_rows.reshape(1, capacity),
        tile_cols.reshape(1, capacity),
        adjacency.reshape(capacity, edge, edge),
    )
    share = 2 * hidden_units // n_col
    piece = max(share // n_row, 8)
    block = (edge, hidden_units)
    dma = pltpu.SemaphoreType.DMA
    results = pl.pallas_call(
        functools.partial(layer_kernel, n_row, n_col),
        out_shape=(
            jax.ShapeDtypeStruct(block, BF16),
            jax.ShapeDtypeStruct(block, BF16),
            jax.ShapeDtypeStruct(self_weight.shape, F32),
            jax.ShapeDtypeStruct(neigh_weight.shape, F32),
        ),
        in_specs=[vmem] * 6,
        out_specs=(vmem,) * 4,
        scratch_shapes=[
            pltpu.VMEM((n_col,) + block, BF16),
            pltpu.VMEM((n_row,) + block, BF16),
            pltpu.VMEM((n_row,) + block, BF16),
            pltpu.VMEM((n_row,) + block, BF16),
            pltpu.VMEM((n_col,) + block, BF16),
            pltpu.VMEM((n_col,) + block, BF16),
            pltpu.VMEM((n_col, share, hidden_units), F32),
            pltpu.VMEM((n_col, share, hidden_units), F32),
            pltpu.VMEM((n_row, piece, hidden_units), F32),
            pltpu.VMEM((n_row, piece, hidden_units), F32),
            pltpu.VMEM((n_row, piece, hidden_units), F32),
            pltpu.VMEM((n_col, share, hidden_units), BF16),
            pltpu.VMEM((hidden_units, cols), F32),
            dma((n_col,)), dma((n_col,)),
            dma((n_row,)), dma((n_row,)),
            dma((n_row,)), dma((n_row,)),
            dma((n_col,)), dma((n_col,)),
            dma((n_col,)), dma((n_col,)),
            dma((n_row,)), dma((n_row,)),
            dma((n_row,)), dma((n_row,)),
            dma((n_col,)), dma((n_col,)),
        ],
        compiler_params=pltpu.CompilerParams(
            collective_id=0, has_side_effects=True, vmem_limit_bytes=32 * 2**20),
        name="layer_exchange",
    )(features, cotangent, self_weight, neigh_weight, degrees.reshape(1, edge), dense)
    return pl.pallas_call(
        finish_kernel,
        out_shape=tuple(jax.ShapeDtypeStruct(x.shape, x.dtype) for x in results),
        in_specs=[vmem] * 4,
        out_specs=(hbm,) * 4,
        scratch_shapes=[dma((4,))],
        name="write_outputs",
    )(*results)


def solution(mesh):
    in_specs = (
        P(("row", "col"), None),
        P(("row", "col"), None),
        P(),
        P(),
        P(("row", "col")),
        P("row", "col", None, None, None),
        P("row", "col", None),
        P("row", "col", None),
        P("row", "col"),
    )
    out_specs = (P(("row", "col"), None), P(("row", "col"), None), P(), P())
    n_row, n_col = mesh.shape["row"], mesh.shape["col"]
    return jax.shard_map(functools.partial(body, n_row, n_col), mesh=mesh,
                         in_specs=in_specs, out_specs=out_specs, check_vma=False)
```

```python
import functools

import jax
import jax.numpy as jnp
from jax import lax
from jax.experimental import pallas as pl
from jax.experimental.pallas import tpu as pltpu
from jax.sharding import PartitionSpec as P

MESH = pl.DeviceIdType.MESH
BF16 = jnp.bfloat16
F32 = jnp.float32
STEP = 4


def dot(a, b, contract=((1,), (0,))):
    return lax.dot_general(a, b, (contract, ((), ())), preferred_element_type=F32)


def each(low, high, step):
    if high - low <= 8:
        for index in range(low, high):
            step(index)
    else:
        def looped(index, carry):
            step(index)
            return carry
        lax.fori_loop(low, high, looped, 0)


def finish_kernel(*refs):
    count = len(refs) // 2
    sems = refs[-1]
    copies = [pltpu.make_async_copy(refs[i], refs[count + i], sems.at[i]) for i in range(count)]
    for copy in copies:
        copy.start()
    for copy in copies:
        copy.wait()


def layer_kernel(
    n_row, n_col,
    order_ref, bounds_ref, feat_ref, cot_ref, self_ref, neigh_ref, deg_ref, tiles_hbm,
    hidden_ref, gfeat_ref, gself_ref, gneigh_ref,
    tiles, sums, dense, src, part_out, part_in, gm, back_out, back_in, w_out, w_in, q_out, q_in, fin, back_acc,
    tiles_r, src_s, src_r, part_s, part_r, gm_s, gm_r, back_s, back_r,
    w_s, w_r, q_s, q_r, fin_s, fin_r,
):
    r = lax.axis_index("row")
    c = lax.axis_index("col")
    edge = feat_ref.shape[0]

    def row_at(d):
        return lax.rem(r + d, n_row)

    def col_at(d):
        return lax.rem(c + d, n_col)

    def over_row(source, target, send, recv, d):
        return pltpu.make_async_remote_copy(
            src_ref=source, dst_ref=target, send_sem=send.at[d], recv_sem=recv.at[d],
            device_id=(row_at(d), c), device_id_type=MESH)

    def over_col(source, target, send, recv, d):
        return pltpu.make_async_remote_copy(
            src_ref=source, dst_ref=target, send_sem=send.at[d], recv_sem=recv.at[d],
            device_id=(r, col_at(d)), device_id_type=MESH)

    fetch = pltpu.make_async_copy(tiles_hbm, tiles, tiles_r)
    fetch.start()
    barrier = pltpu.get_barrier_semaphore()
    each(1, n_col, lambda d: pl.semaphore_signal(
        barrier, inc=1, device_id=(r, col_at(d)), device_id_type=MESH))
    each(1, n_row, lambda d: pl.semaphore_signal(
        barrier, inc=1, device_id=(row_at(d), c), device_id_type=MESH))
    pl.semaphore_wait(barrier, n_row + n_col - 2)

    def src_copy(d):
        return over_col(feat_ref, src.at[c], src_s, src_r, d)

    each(1, n_col, lambda d: src_copy(d).start())
    keep = pltpu.make_async_copy(feat_ref, src.at[c], src_r.at[0])
    keep.start()
    inv_row = lax.rsqrt(jnp.maximum(deg_ref[...], 1).astype(F32))
    down = lax.broadcasted_iota(jnp.int32, (edge, edge), 0)
    across = lax.broadcasted_iota(jnp.int32, (edge, edge), 1)
    inv_col = jnp.sum(jnp.where(down == across, inv_row, 0.0), axis=1, keepdims=True)
    own_linear = dot(feat_ref[...], self_ref[...])
    fetch.wait()

    capacity = tiles.shape[0]
    sums[0] = jnp.zeros(sums.shape[1:], BF16)

    def run(step, total):
        for k in range(STEP):
            slot = step * STEP + k
            total = total + tiles[order_ref[0, slot]].astype(F32).astype(BF16)
            sums[slot + 1] = total
        return total

    lax.fori_loop(0, capacity // STEP, run, jnp.zeros(sums.shape[1:], BF16))

    def place(row, carry):
        for col in range(n_col):
            spot = row * n_col + col
            rows = pl.ds(pl.multiple_of(row * edge, edge), edge)
            dense[rows, col * edge:(col + 1) * edge] = (
                sums[bounds_ref[0, spot + 1]] - sums[bounds_ref[0, spot]])
        return carry

    lax.fori_loop(0, n_row, place, 0)
    keep.wait()
    each(1, n_col, lambda d: src_copy(d).wait_recv())
    source = src[...].reshape(n_col * edge, src.shape[-1])

    def part_copy(d):
        return over_row(part_out.at[d], part_in.at[d], part_s, part_r, d)

    def partial(d):
        rows = pl.ds(pl.multiple_of(row_at(d) * edge, edge), edge)
        return dot(dense[rows, :], source)

    def send_part(d):
        part_out[d] = partial(d).astype(BF16)
        part_copy(d).start()

    each(1, n_row, send_part)
    agg = partial(0).astype(BF16).astype(F32)
    for d in range(1, n_row):
        part_copy(d).wait_recv()
        agg = agg + part_in[d].astype(F32)

    mixed = (agg * inv_col).astype(BF16)
    linear = own_linear + dot(mixed, neigh_ref[...])
    sigma = jax.nn.sigmoid(linear)
    slope = sigma * (1.0 + linear * (1.0 - sigma))
    grad_linear = (cot_ref[...].astype(F32) * slope).astype(BF16)
    gm[r] = (dot(neigh_ref[...], grad_linear, ((1,), (1,))) * inv_row).astype(BF16)

    def gm_copy(d):
        return over_row(gm.at[r], gm.at[r], gm_s, gm_r, d)

    each(1, n_row, lambda d: gm_copy(d).start())

    share = w_out.shape[1]
    both = jnp.concatenate([feat_ref[...], mixed], axis=1)
    w_out[...] = dot(both, grad_linear, ((0,), (0,))).reshape(w_out.shape)

    def w_copy(d):
        return over_col(w_out.at[col_at(d)], w_in.at[d], w_s, w_r, d)

    each(1, n_col, lambda d: w_copy(d).start())
    hidden_ref[...] = (linear * sigma).astype(BF16)
    own_grad = dot(grad_linear, self_ref[...], ((1,), (1,)))

    def q_copy(d):
        return over_row(q_out, q_in.at[d], q_s, q_r, d)

    def sum_over_col():
        total = w_out[c]
        for d in range(1, n_col):
            w_copy(d).wait_recv()
            total = total + w_in[d]
        q_out[...] = total.astype(BF16)
        each(1, n_row, lambda d: q_copy(d).start())
        return total

    def back_term(d):
        owner = lax.rem(r - d + n_row, n_row)
        rows = pl.ds(pl.multiple_of(owner * edge, edge), edge)
        return dot(gm[owner], dense[rows, :])

    def add_back(d):
        gm_copy(d).wait_recv()
        back_acc[...] += back_term(d)

    middle = (n_row + 1) // 2
    back_acc[...] = back_term(0)
    each(1, middle, add_back)
    total = sum_over_col()
    each(middle, n_row, add_back)

    for b in range(n_col):
        back_out[b] = back_acc[:, b * edge:(b + 1) * edge].astype(BF16)

    def back_copy(d):
        return over_col(back_out.at[col_at(d)], back_in.at[d], back_s, back_r, d)

    each(1, n_col, lambda d: back_copy(d).start())

    for d in range(1, n_row):
        q_copy(d).wait_recv()
        total = total + q_in[d].astype(F32)
    fin[c] = total.astype(BF16)

    def fin_copy(d):
        return over_col(fin.at[c], fin.at[c], fin_s, fin_r, d)

    each(1, n_col, lambda d: fin_copy(d).start())
    returned = back_out[c].astype(F32)
    for d in range(1, n_col):
        back_copy(d).wait_recv()
        returned = returned + back_in[d].astype(F32)
    gfeat_ref[...] = (own_grad + returned.T).astype(BF16)

    each(1, n_col, lambda d: fin_copy(d).wait_recv())
    grads = fin[...].reshape(n_col * share, fin.shape[-1]).astype(F32)
    half = gself_ref.shape[0]
    gself_ref[...] = grads[:half]
    gneigh_ref[...] = grads[half:]

    def drain_col(d):
        for copy in (src_copy, w_copy, back_copy, fin_copy):
            copy(d).wait_send()

    def drain_row(d):
        for copy in (part_copy, gm_copy, q_copy):
            copy(d).wait_send()

    each(1, n_col, drain_col)
    each(1, n_row, drain_row)


def body(n_row, n_col, features, cotangent, self_weight, neigh_weight, degrees,
         adjacency, tile_rows, tile_cols, tile_count):
    edge = adjacency.shape[-1]
    capacity = adjacency.shape[2]
    hidden_units = features.shape[-1]
    rows, cols = n_row * edge, n_col * edge
    smem = pl.BlockSpec(memory_space=pltpu.SMEM)
    vmem = pl.BlockSpec(memory_space=pltpu.VMEM)
    hbm = pl.BlockSpec(memory_space=pltpu.HBM)
    places = n_row * n_col
    slots = jnp.arange(capacity, dtype=jnp.int32)
    keys = jnp.where(slots < tile_count.reshape(()),
                     tile_rows.reshape(capacity) * n_col + tile_cols.reshape(capacity), places)
    spots = jnp.arange(places + 1, dtype=jnp.int32)
    bounds = jnp.sum((keys[None, :] < spots[:, None]).astype(jnp.int32), axis=1)
    ahead = (keys[None, :] < keys[:, None]) | (
        (keys[None, :] == keys[:, None]) & (slots[None, :] < slots[:, None]))
    rank = jnp.sum(ahead.astype(jnp.int32), axis=1)
    order = jnp.sum(jnp.where(rank[None, :] == slots[:, None], slots[None, :], 0), axis=1)
    share = 2 * hidden_units // n_col
    block = (edge, hidden_units)
    dma = pltpu.SemaphoreType.DMA
    results = pl.pallas_call(
        functools.partial(layer_kernel, n_row, n_col),
        out_shape=(
            jax.ShapeDtypeStruct(block, BF16),
            jax.ShapeDtypeStruct(block, BF16),
            jax.ShapeDtypeStruct(self_weight.shape, F32),
            jax.ShapeDtypeStruct(neigh_weight.shape, F32),
        ),
        in_specs=[smem] * 2 + [vmem] * 5 + [hbm],
        out_specs=(vmem,) * 4,
        scratch_shapes=[
            pltpu.VMEM((capacity, edge, edge), jnp.int32),
            pltpu.VMEM((capacity + 1, edge, edge), BF16),
            pltpu.VMEM((rows, cols), BF16),
            pltpu.VMEM((n_col,) + block, BF16),
            pltpu.VMEM((n_row,) + block, BF16),
            pltpu.VMEM((n_row,) + block, BF16),
            pltpu.VMEM((n_row,) + block, BF16),
            pltpu.VMEM((n_col,) + block, BF16),
            pltpu.VMEM((n_col,) + block, BF16),
            pltpu.VMEM((n_col, share, hidden_units), F32),
            pltpu.VMEM((n_col, share, hidden_units), F32),
            pltpu.VMEM((share, hidden_units), BF16),
            pltpu.VMEM((n_row, share, hidden_units), BF16),
            pltpu.VMEM((n_col, share, hidden_units), BF16),
            pltpu.VMEM((hidden_units, cols), F32),
            dma,
            dma((n_col,)), dma((n_col,)),
            dma((n_row,)), dma((n_row,)),
            dma((n_row,)), dma((n_row,)),
            dma((n_col,)), dma((n_col,)),
            dma((n_col,)), dma((n_col,)),
            dma((n_row,)), dma((n_row,)),
            dma((n_col,)), dma((n_col,)),
        ],
        compiler_params=pltpu.CompilerParams(
            collective_id=0, has_side_effects=True, vmem_limit_bytes=58 * 2**20),
        name="layer_exchange",
    )(order.reshape(1, capacity), bounds.reshape(1, places + 1), features, cotangent,
      self_weight, neigh_weight, degrees.reshape(1, edge),
      adjacency.reshape(capacity, edge, edge))
    return pl.pallas_call(
        finish_kernel,
        out_shape=tuple(jax.ShapeDtypeStruct(x.shape, x.dtype) for x in results),
        in_specs=[hbm] * 4,
        out_specs=(hbm,) * 4,
        scratch_shapes=[dma((4,))],
        compiler_params=pltpu.CompilerParams(vmem_limit_bytes=60 * 2**20),
        name="write_outputs",
    )(*results)


def solution(mesh):
    in_specs = (
        P(("row", "col"), None),
        P(("row", "col"), None),
        P(),
        P(),
        P(("row", "col")),
        P("row", "col", None, None, None),
        P("row", "col", None),
        P("row", "col", None),
        P("row", "col"),
    )
    out_specs = (P(("row", "col"), None), P(("row", "col"), None), P(), P())
    n_row, n_col = mesh.shape["row"], mesh.shape["col"]
    return jax.shard_map(functools.partial(body, n_row, n_col), mesh=mesh,
                         in_specs=in_specs, out_specs=out_specs, check_vma=False)
```

```python
import functools

import jax
import jax.numpy as jnp
from jax import lax
from jax.experimental import pallas as pl
from jax.experimental.pallas import tpu as pltpu
from jax.sharding import PartitionSpec as P

MESH = pl.DeviceIdType.MESH
BF16 = jnp.bfloat16
F32 = jnp.float32
STEP = 4


def dot(a, b, contract=((1,), (0,))):
    return lax.dot_general(a, b, (contract, ((), ())), preferred_element_type=F32)


def each(low, high, step):
    if high - low <= 8:
        for index in range(low, high):
            step(index)
    else:
        def looped(index, carry):
            step(index)
            return carry
        lax.fori_loop(low, high, looped, 0)


def finish_kernel(*refs):
    count = len(refs) // 2
    for i in range(count):
        refs[count + i][...] = refs[i][...]


def layer_kernel(
    n_row, n_col,
    count_ref, rows_ref, cols_ref, feat_ref, cot_ref, self_ref, neigh_ref, deg_ref, tiles_hbm,
    hidden_ref, gfeat_ref, gself_ref, gneigh_ref,
    slot_lists, order_ref, bounds_ref, tiles, sums, dense, src, part_out, part_in, gm, back_out, back_in, w_out, w_in, q_out, q_in, fin, back_acc,
    lists_r, tiles_r, src_s, src_r, part_s, part_r, gm_s, gm_r, back_s, back_r,
    w_s, w_r, q_s, q_r, fin_s, fin_r,
):
    r = lax.axis_index("row")
    c = lax.axis_index("col")
    edge = feat_ref.shape[0]

    def row_at(d):
        return lax.rem(r + d, n_row)

    def col_at(d):
        return lax.rem(c + d, n_col)

    def over_row(source, target, send, recv, d):
        return pltpu.make_async_remote_copy(
            src_ref=source, dst_ref=target, send_sem=send.at[d], recv_sem=recv.at[d],
            device_id=(row_at(d), c), device_id_type=MESH)

    def over_col(source, target, send, recv, d):
        return pltpu.make_async_remote_copy(
            src_ref=source, dst_ref=target, send_sem=send.at[d], recv_sem=recv.at[d],
            device_id=(r, col_at(d)), device_id_type=MESH)

    fetch = pltpu.make_async_copy(tiles_hbm, tiles, tiles_r)
    fetch.start()
    barrier = pltpu.get_barrier_semaphore()
    each(1, n_col, lambda d: pl.semaphore_signal(
        barrier, inc=1, device_id=(r, col_at(d)), device_id_type=MESH))
    each(1, n_row, lambda d: pl.semaphore_signal(
        barrier, inc=1, device_id=(row_at(d), c), device_id_type=MESH))

    capacity = tiles.shape[0]
    places = n_row * n_col
    slot_down = lax.broadcasted_iota(jnp.int32, (capacity, capacity), 0)
    slot_across = lax.broadcasted_iota(jnp.int32, (capacity, capacity), 1)
    key_row = jnp.where(slot_across[:1] < count_ref[...],
                        rows_ref[...] * n_col + cols_ref[...], places)
    key_col = jnp.sum(jnp.where(slot_down == slot_across, key_row, 0), axis=1, keepdims=True)
    ahead = (key_row < key_col) | ((key_row == key_col) & (slot_across < slot_down))
    rank = jnp.sum(jnp.where(ahead, 1, 0), axis=1, keepdims=True)
    slot_lists[0:1, :capacity] = jnp.sum(
        jnp.where(rank == slot_across, slot_down, 0), axis=0, keepdims=True)
    spots = lax.broadcasted_iota(jnp.int32, (capacity, slot_lists.shape[1]), 1)
    slot_lists[1:2, :] = jnp.sum(jnp.where(key_col < spots, 1, 0), axis=0, keepdims=True)
    lists = [pltpu.make_async_copy(slot_lists.at[pl.ds(i, 1)], ref, lists_r.at[i])
             for i, ref in enumerate((order_ref, bounds_ref))]
    for copy in lists:
        copy.start()
    pl.semaphore_wait(barrier, n_row + n_col - 2)

    def src_copy(d):
        return over_col(feat_ref, src.at[c], src_s, src_r, d)

    each(1, n_col, lambda d: src_copy(d).start())
    keep = pltpu.make_async_copy(feat_ref, src.at[c], src_r.at[0])
    keep.start()
    inv_row = lax.rsqrt(jnp.maximum(deg_ref[...], 1).astype(F32))
    down = lax.broadcasted_iota(jnp.int32, (edge, edge), 0)
    across = lax.broadcasted_iota(jnp.int32, (edge, edge), 1)
    inv_col = jnp.sum(jnp.where(down == across, inv_row, 0.0), axis=1, keepdims=True)
    own_linear = dot(feat_ref[...], self_ref[...])
    for copy in lists:
        copy.wait()
    fetch.wait()

    sums[0] = jnp.zeros(sums.shape[1:], BF16)

    def run(step, total):
        for k in range(STEP):
            slot = step * STEP + k
            total = total + tiles[order_ref[0, slot]].astype(F32).astype(BF16)
            sums[slot + 1] = total
        return total

    lax.fori_loop(0, capacity // STEP, run, jnp.zeros(sums.shape[1:], BF16))

    def place(row, carry):
        for col in range(n_col):
            spot = row * n_col + col
            rows = pl.ds(pl.multiple_of(row * edge, edge), edge)
            dense[rows, col * edge:(col + 1) * edge] = (
                sums[bounds_ref[0, spot + 1]] - sums[bounds_ref[0, spot]])
        return carry

    lax.fori_loop(0, n_row, place, 0)
    keep.wait()
    each(1, n_col, lambda d: src_copy(d).wait_recv())
    source = src[...].reshape(n_col * edge, src.shape[-1])

    def part_copy(d):
        return over_row(part_out.at[d], part_in.at[d], part_s, part_r, d)

    def partial(d):
        rows = pl.ds(pl.multiple_of(row_at(d) * edge, edge), edge)
        return dot(dense[rows, :], source)

    def send_part(d):
        part_out[d] = partial(d).astype(BF16)
        part_copy(d).start()

    each(1, n_row, send_part)
    agg = partial(0).astype(BF16).astype(F32)
    for d in range(1, n_row):
        part_copy(d).wait_recv()
        agg = agg + part_in[d].astype(F32)

    mixed = (agg * inv_col).astype(BF16)
    linear = own_linear + dot(mixed, neigh_ref[...])
    sigma = jax.nn.sigmoid(linear)
    slope = sigma * (1.0 + linear * (1.0 - sigma))
    grad_linear = (cot_ref[...].astype(F32) * slope).astype(BF16)
    gm[r] = (dot(neigh_ref[...], grad_linear, ((1,), (1,))) * inv_row).astype(BF16)

    def gm_copy(d):
        return over_row(gm.at[r], gm.at[r], gm_s, gm_r, d)

    each(1, n_row, lambda d: gm_copy(d).start())

    share = w_out.shape[1]
    both = jnp.concatenate([feat_ref[...], mixed], axis=1)
    w_out[...] = dot(both, grad_linear, ((0,), (0,))).reshape(w_out.shape)

    def w_copy(d):
        return over_col(w_out.at[col_at(d)], w_in.at[d], w_s, w_r, d)

    each(1, n_col, lambda d: w_copy(d).start())
    hidden_ref[...] = (linear * sigma).astype(BF16)
    own_grad = dot(grad_linear, self_ref[...], ((1,), (1,)))

    def q_copy(d):
        return over_row(q_out, q_in.at[d], q_s, q_r, d)

    def sum_over_col():
        total = w_out[c]
        for d in range(1, n_col):
            w_copy(d).wait_recv()
            total = total + w_in[d]
        q_out[...] = total.astype(BF16)
        each(1, n_row, lambda d: q_copy(d).start())
        return total

    def back_term(d):
        owner = lax.rem(r - d + n_row, n_row)
        rows = pl.ds(pl.multiple_of(owner * edge, edge), edge)
        return dot(gm[owner], dense[rows, :])

    def add_back(d):
        gm_copy(d).wait_recv()
        back_acc[...] += back_term(d)

    back_acc[...] = back_term(0)
    total = sum_over_col()
    each(1, n_row, add_back)

    for b in range(n_col):
        back_out[b] = back_acc[:, b * edge:(b + 1) * edge].astype(BF16)

    def back_copy(d):
        return over_col(back_out.at[col_at(d)], back_in.at[d], back_s, back_r, d)

    each(1, n_col, lambda d: back_copy(d).start())

    for d in range(1, n_row):
        q_copy(d).wait_recv()
        total = total + q_in[d].astype(F32)
    fin[c] = total.astype(BF16)

    def fin_copy(d):
        return over_col(fin.at[c], fin.at[c], fin_s, fin_r, d)

    each(1, n_col, lambda d: fin_copy(d).start())
    returned = back_out[c].astype(F32)
    for d in range(1, n_col):
        back_copy(d).wait_recv()
        returned = returned + back_in[d].astype(F32)
    gfeat_ref[...] = (own_grad + returned.T).astype(BF16)

    each(1, n_col, lambda d: fin_copy(d).wait_recv())
    grads = fin[...].reshape(n_col * share, fin.shape[-1]).astype(F32)
    half = gself_ref.shape[0]
    gself_ref[...] = grads[:half]
    gneigh_ref[...] = grads[half:]

    def drain_col(d):
        for copy in (src_copy, w_copy, back_copy, fin_copy):
            copy(d).wait_send()

    def drain_row(d):
        for copy in (part_copy, gm_copy, q_copy):
            copy(d).wait_send()

    each(1, n_col, drain_col)
    each(1, n_row, drain_row)


def body(n_row, n_col, features, cotangent, self_weight, neigh_weight, degrees,
         adjacency, tile_rows, tile_cols, tile_count):
    edge = adjacency.shape[-1]
    capacity = adjacency.shape[2]
    hidden_units = features.shape[-1]
    rows, cols = n_row * edge, n_col * edge
    vmem = pl.BlockSpec(memory_space=pltpu.VMEM)
    hbm = pl.BlockSpec(memory_space=pltpu.HBM)
    list_width = -(-(n_row * n_col + 1) // 128) * 128
    share = 2 * hidden_units // n_col
    block = (edge, hidden_units)
    dma = pltpu.SemaphoreType.DMA
    results = pl.pallas_call(
        functools.partial(layer_kernel, n_row, n_col),
        out_shape=(
            jax.ShapeDtypeStruct(block, BF16),
            jax.ShapeDtypeStruct(block, BF16),
            jax.ShapeDtypeStruct(self_weight.shape, F32),
            jax.ShapeDtypeStruct(neigh_weight.shape, F32),
        ),
        in_specs=[vmem] * 8 + [hbm],
        out_specs=(vmem,) * 4,
        scratch_shapes=[
            pltpu.VMEM((8, list_width), jnp.int32),
            pltpu.SMEM((1, list_width), jnp.int32),
            pltpu.SMEM((1, list_width), jnp.int32),
            pltpu.VMEM((capacity, edge, edge), jnp.int32),
            pltpu.VMEM((capacity + 1, edge, edge), BF16),
            pltpu.VMEM((rows, cols), BF16),
            pltpu.VMEM((n_col,) + block, BF16),
            pltpu.VMEM((n_row,) + block, BF16),
            pltpu.VMEM((n_row,) + block, BF16),
            pltpu.VMEM((n_row,) + block, BF16),
            pltpu.VMEM((n_col,) + block, BF16),
            pltpu.VMEM((n_col,) + block, BF16),
            pltpu.VMEM((n_col, share, hidden_units), F32),
            pltpu.VMEM((n_col, share, hidden_units), F32),
            pltpu.VMEM((share, hidden_units), BF16),
            pltpu.VMEM((n_row, share, hidden_units), BF16),
            pltpu.VMEM((n_col, share, hidden_units), BF16),
            pltpu.VMEM((hidden_units, cols), F32),
            dma((2,)),
            dma,
            dma((n_col,)), dma((n_col,)),
            dma((n_row,)), dma((n_row,)),
            dma((n_row,)), dma((n_row,)),
            dma((n_col,)), dma((n_col,)),
            dma((n_col,)), dma((n_col,)),
            dma((n_row,)), dma((n_row,)),
            dma((n_col,)), dma((n_col,)),
        ],
        compiler_params=pltpu.CompilerParams(
            collective_id=0, has_side_effects=True, vmem_limit_bytes=58 * 2**20),
        name="layer_exchange",
    )(tile_count.reshape(1, 1), tile_rows.reshape(1, capacity), tile_cols.reshape(1, capacity),
      features, cotangent, self_weight, neigh_weight, degrees.reshape(1, edge),
      adjacency.reshape(capacity, edge, edge))
    return pl.pallas_call(
        finish_kernel,
        out_shape=tuple(jax.ShapeDtypeStruct(x.shape, x.dtype) for x in results),
        in_specs=[vmem] * 4,
        out_specs=(vmem,) * 4,
        compiler_params=pltpu.CompilerParams(vmem_limit_bytes=60 * 2**20),
        name="write_outputs",
    )(*results)


def solution(mesh):
    in_specs = (
        P(("row", "col"), None),
        P(("row", "col"), None),
        P(),
        P(),
        P(("row", "col")),
        P("row", "col", None, None, None),
        P("row", "col", None),
        P("row", "col", None),
        P("row", "col"),
    )
    out_specs = (P(("row", "col"), None), P(("row", "col"), None), P(), P())
    n_row, n_col = mesh.shape["row"], mesh.shape["col"]
    return jax.shard_map(functools.partial(body, n_row, n_col), mesh=mesh,
                         in_specs=in_specs, out_specs=out_specs, check_vma=False)
```

```python
import functools

import jax
import jax.numpy as jnp
from jax import lax
from jax.experimental import pallas as pl
from jax.experimental.pallas import tpu as pltpu
from jax.sharding import PartitionSpec as P

MESH = pl.DeviceIdType.MESH
BF16 = jnp.bfloat16
F32 = jnp.float32
STEP = 4


def dot(a, b, contract=((1,), (0,))):
    return lax.dot_general(a, b, (contract, ((), ())), preferred_element_type=F32)


def each(low, high, step):
    if high - low <= 8:
        for index in range(low, high):
            step(index)
    else:
        def looped(index, carry):
            step(index)
            return carry
        lax.fori_loop(low, high, looped, 0)


def finish_kernel(*refs):
    count = len(refs) // 2
    for i in range(count):
        refs[count + i][...] = refs[i][...]


def layer_kernel(
    n_row, n_col,
    count_ref, rows_ref, cols_ref, feat_ref, cot_ref, self_ref, neigh_ref, deg_ref, tiles_hbm,
    hidden_ref, gfeat_ref, gself_ref, gneigh_ref,
    slot_lists, order_ref, bounds_ref, tiles, sums, dense, src, px_out, px_in, pz_out, pz_in, gm, back_out, back_in, w_out, w_in, qx_out, qx_in, qz_out, qz_in, fin, back_acc,
    lists_r, tiles_r, src_s, src_r, px_s, px_r, pz_s, pz_r, gm_s, gm_r, fw_s, fw_r, back_s, back_r,
    w_s, w_r, qx_s, qx_r, qz_s, qz_r, fin_s, fin_r,
):
    r = lax.axis_index("row")
    c = lax.axis_index("col")
    edge = feat_ref.shape[0]

    n_line = n_row // 2
    line, side = r // 2, lax.rem(r, 2)

    def ahead_of(e):
        return lax.rem(line + e, n_line)

    def behind(e):
        return lax.rem(line - e + n_line, n_line)

    def col_at(d):
        return lax.rem(c + d, n_col)

    def over_pair(source, target, send, recv):
        return pltpu.make_async_remote_copy(
            src_ref=source, dst_ref=target, send_sem=send, recv_sem=recv,
            device_id=(line * 2 + 1 - side, c), device_id_type=MESH)

    def over_line(source, target, send, recv, e):
        return pltpu.make_async_remote_copy(
            src_ref=source, dst_ref=target, send_sem=send.at[e], recv_sem=recv.at[e],
            device_id=(ahead_of(e) * 2 + side, c), device_id_type=MESH)

    def over_col(source, target, send, recv, d):
        return pltpu.make_async_remote_copy(
            src_ref=source, dst_ref=target, send_sem=send.at[d], recv_sem=recv.at[d],
            device_id=(r, col_at(d)), device_id_type=MESH)

    fetch = pltpu.make_async_copy(tiles_hbm, tiles, tiles_r)
    fetch.start()
    barrier = pltpu.get_barrier_semaphore()
    each(1, n_col, lambda d: pl.semaphore_signal(
        barrier, inc=1, device_id=(r, col_at(d)), device_id_type=MESH))
    pl.semaphore_signal(
        barrier, inc=1, device_id=(line * 2 + 1 - side, c), device_id_type=MESH)
    each(1, n_line, lambda e: pl.semaphore_signal(
        barrier, inc=1, device_id=(ahead_of(e) * 2 + side, c), device_id_type=MESH))

    capacity = tiles.shape[0]
    places = n_row * n_col
    slot_down = lax.broadcasted_iota(jnp.int32, (capacity, capacity), 0)
    slot_across = lax.broadcasted_iota(jnp.int32, (capacity, capacity), 1)
    key_row = jnp.where(slot_across[:1] < count_ref[...],
                        rows_ref[...] * n_col + cols_ref[...], places)
    key_col = jnp.sum(jnp.where(slot_down == slot_across, key_row, 0), axis=1, keepdims=True)
    ahead = (key_row < key_col) | ((key_row == key_col) & (slot_across < slot_down))
    rank = jnp.sum(jnp.where(ahead, 1, 0), axis=1, keepdims=True)
    slot_lists[0:1, :capacity] = jnp.sum(
        jnp.where(rank == slot_across, slot_down, 0), axis=0, keepdims=True)
    spots = lax.broadcasted_iota(jnp.int32, (capacity, slot_lists.shape[1]), 1)
    slot_lists[1:2, :] = jnp.sum(jnp.where(key_col < spots, 1, 0), axis=0, keepdims=True)
    lists = [pltpu.make_async_copy(slot_lists.at[pl.ds(i, 1)], ref, lists_r.at[i])
             for i, ref in enumerate((order_ref, bounds_ref))]
    for copy in lists:
        copy.start()
    pl.semaphore_wait(barrier, n_line + n_col - 1)

    def src_copy(d):
        return over_col(feat_ref, src.at[c], src_s, src_r, d)

    each(1, n_col, lambda d: src_copy(d).start())
    keep = pltpu.make_async_copy(feat_ref, src.at[c], src_r.at[0])
    keep.start()
    inv_row = lax.rsqrt(jnp.maximum(deg_ref[...], 1).astype(F32))
    down = lax.broadcasted_iota(jnp.int32, (edge, edge), 0)
    across = lax.broadcasted_iota(jnp.int32, (edge, edge), 1)
    inv_col = jnp.sum(jnp.where(down == across, inv_row, 0.0), axis=1, keepdims=True)
    own_linear = dot(feat_ref[...], self_ref[...])
    for copy in lists:
        copy.wait()
    fetch.wait()

    sums[0] = jnp.zeros(sums.shape[1:], BF16)

    def run(step, total):
        for k in range(STEP):
            slot = step * STEP + k
            total = total + tiles[order_ref[0, slot]].astype(F32).astype(BF16)
            sums[slot + 1] = total
        return total

    lax.fori_loop(0, capacity // STEP, run, jnp.zeros(sums.shape[1:], BF16))

    def place(row, carry):
        for col in range(n_col):
            spot = row * n_col + col
            rows = pl.ds(pl.multiple_of(row * edge, edge), edge)
            dense[rows, col * edge:(col + 1) * edge] = (
                sums[bounds_ref[0, spot + 1]] - sums[bounds_ref[0, spot]])
        return carry

    lax.fori_loop(0, n_row, place, 0)
    keep.wait()
    each(1, n_col, lambda d: src_copy(d).wait_recv())
    source = src[...].reshape(n_col * edge, src.shape[-1])

    def px_copy(e):
        return over_pair(px_out.at[e], px_in.at[e], px_s.at[e], px_r.at[e])

    def pz_copy(e):
        return over_line(pz_out.at[e], pz_in.at[e], pz_s, pz_r, e)

    def partial(e, which):
        rows = pl.ds(pl.multiple_of((ahead_of(e) * 2 + which) * edge, edge), edge)
        return dot(dense[rows, :], source)

    def send_px(e):
        px_out[e] = partial(e, 1 - side).astype(BF16)
        px_copy(e).start()

    def send_pz(e):
        own = partial(e, side)
        px_copy(e).wait_recv()
        pz_out[e] = (own + px_in[e].astype(F32)).astype(BF16)
        pz_copy(e).start()

    each(1, n_line, send_px)
    send_px(0)
    each(1, n_line, send_pz)
    agg = partial(0, side)
    px_copy(0).wait_recv()
    agg = agg + px_in[0].astype(F32)
    for e in range(1, n_line):
        pz_copy(e).wait_recv()
        agg = agg + pz_in[e].astype(F32)

    mixed = (agg * inv_col).astype(BF16)
    linear = own_linear + dot(mixed, neigh_ref[...])
    sigma = jax.nn.sigmoid(linear)
    slope = sigma * (1.0 + linear * (1.0 - sigma))
    grad_linear = (cot_ref[...].astype(F32) * slope).astype(BF16)
    gm[r] = (dot(neigh_ref[...], grad_linear, ((1,), (1,))) * inv_row).astype(BF16)

    def gm_copy(e):
        return over_line(gm.at[r], gm.at[r], gm_s, gm_r, e)

    def fw_copy(e):
        block = gm.at[behind(e) * 2 + side]
        return over_pair(block, block, fw_s.at[e], fw_r.at[e])

    each(1, n_line, lambda e: gm_copy(e).start())
    fw_copy(0).start()

    share = w_out.shape[1]
    both = jnp.concatenate([feat_ref[...], mixed], axis=1)
    w_out[...] = dot(both, grad_linear, ((0,), (0,))).reshape(w_out.shape)

    def w_copy(d):
        return over_col(w_out.at[col_at(d)], w_in.at[d], w_s, w_r, d)

    each(1, n_col, lambda d: w_copy(d).start())
    hidden_ref[...] = (linear * sigma).astype(BF16)
    own_grad = dot(grad_linear, self_ref[...], ((1,), (1,)))

    qx_copy = over_pair(qx_out, qx_in, qx_s, qx_r)

    def qz_copy(e):
        return over_line(qz_out, qz_in.at[e], qz_s, qz_r, e)

    def forward(e):
        gm_copy(e).wait_recv()
        fw_copy(e).start()

    def back_term(e):
        fw_copy(e).wait_recv()
        first = behind(e) * 2
        rows = pl.ds(pl.multiple_of(first * edge, 2 * edge), 2 * edge)
        return dot(jnp.concatenate([gm[first], gm[first + 1]], axis=1), dense[rows, :])

    def add_back(e):
        back_acc[...] += back_term(e)

    forward(1)
    total = w_out[c]
    for d in range(1, n_col):
        w_copy(d).wait_recv()
        total = total + w_in[d]
    qx_out[...] = total.astype(BF16)
    qx_copy.start()
    back_acc[...] = back_term(0)
    forward(2)
    add_back(1)
    qx_copy.wait_recv()
    total = total + qx_in[...].astype(F32)
    qz_out[...] = total.astype(BF16)
    each(1, n_line, lambda e: qz_copy(e).start())

    def forward_and_add(e):
        forward(e)
        add_back(e - 1)

    each(3, n_line, forward_and_add)
    add_back(n_line - 1)

    for b in range(n_col):
        back_out[b] = back_acc[:, b * edge:(b + 1) * edge].astype(BF16)

    def back_copy(d):
        return over_col(back_out.at[col_at(d)], back_in.at[d], back_s, back_r, d)

    each(1, n_col, lambda d: back_copy(d).start())

    for e in range(1, n_line):
        qz_copy(e).wait_recv()
        total = total + qz_in[e].astype(F32)
    fin[c] = total.astype(BF16)

    def fin_copy(d):
        return over_col(fin.at[c], fin.at[c], fin_s, fin_r, d)

    each(1, n_col, lambda d: fin_copy(d).start())
    returned = back_out[c].astype(F32)
    for d in range(1, n_col):
        back_copy(d).wait_recv()
        returned = returned + back_in[d].astype(F32)
    gfeat_ref[...] = (own_grad + returned.T).astype(BF16)

    each(1, n_col, lambda d: fin_copy(d).wait_recv())
    grads = fin[...].reshape(n_col * share, fin.shape[-1]).astype(F32)
    half = gself_ref.shape[0]
    gself_ref[...] = grads[:half]
    gneigh_ref[...] = grads[half:]

    def drain_col(d):
        for copy in (src_copy, w_copy, back_copy, fin_copy):
            copy(d).wait_send()

    def drain_line(e):
        for copy in (px_copy, pz_copy, gm_copy, fw_copy, qz_copy):
            copy(e).wait_send()

    each(1, n_col, drain_col)
    each(1, n_line, drain_line)
    for copy in (px_copy(0), fw_copy(0), qx_copy):
        copy.wait_send()


def body(n_row, n_col, features, cotangent, self_weight, neigh_weight, degrees,
         adjacency, tile_rows, tile_cols, tile_count):
    edge = adjacency.shape[-1]
    capacity = adjacency.shape[2]
    hidden_units = features.shape[-1]
    rows, cols = n_row * edge, n_col * edge
    vmem = pl.BlockSpec(memory_space=pltpu.VMEM)
    hbm = pl.BlockSpec(memory_space=pltpu.HBM)
    list_width = -(-(n_row * n_col + 1) // 128) * 128
    share = 2 * hidden_units // n_col
    n_line = n_row // 2
    block = (edge, hidden_units)
    dma = pltpu.SemaphoreType.DMA
    results = pl.pallas_call(
        functools.partial(layer_kernel, n_row, n_col),
        out_shape=(
            jax.ShapeDtypeStruct(block, BF16),
            jax.ShapeDtypeStruct(block, BF16),
            jax.ShapeDtypeStruct(self_weight.shape, F32),
            jax.ShapeDtypeStruct(neigh_weight.shape, F32),
        ),
        in_specs=[vmem] * 8 + [hbm],
        out_specs=(vmem,) * 4,
        scratch_shapes=[
            pltpu.VMEM((8, list_width), jnp.int32),
            pltpu.SMEM((1, list_width), jnp.int32),
            pltpu.SMEM((1, list_width), jnp.int32),
            pltpu.VMEM((capacity, edge, edge), jnp.int32),
            pltpu.VMEM((capacity + 1, edge, edge), BF16),
            pltpu.VMEM((rows, cols), BF16),
            pltpu.VMEM((n_col,) + block, BF16),
            pltpu.VMEM((n_line,) + block, BF16),
            pltpu.VMEM((n_line,) + block, BF16),
            pltpu.VMEM((n_line,) + block, BF16),
            pltpu.VMEM((n_line,) + block, BF16),
            pltpu.VMEM((n_row,) + block, BF16),
            pltpu.VMEM((n_col,) + block, BF16),
            pltpu.VMEM((n_col,) + block, BF16),
            pltpu.VMEM((n_col, share, hidden_units), F32),
            pltpu.VMEM((n_col, share, hidden_units), F32),
            pltpu.VMEM((share, hidden_units), BF16),
            pltpu.VMEM((share, hidden_units), BF16),
            pltpu.VMEM((share, hidden_units), BF16),
            pltpu.VMEM((n_line, share, hidden_units), BF16),
            pltpu.VMEM((n_col, share, hidden_units), BF16),
            pltpu.VMEM((hidden_units, cols), F32),
            dma((2,)),
            dma,
            dma((n_col,)), dma((n_col,)),
            dma((n_line,)), dma((n_line,)),
            dma((n_line,)), dma((n_line,)),
            dma((n_line,)), dma((n_line,)),
            dma((n_line,)), dma((n_line,)),
            dma((n_col,)), dma((n_col,)),
            dma((n_col,)), dma((n_col,)),
            dma, dma,
            dma((n_line,)), dma((n_line,)),
            dma((n_col,)), dma((n_col,)),
        ],
        compiler_params=pltpu.CompilerParams(
            collective_id=0, has_side_effects=True, vmem_limit_bytes=58 * 2**20),
        name="layer_exchange",
    )(tile_count.reshape(1, 1), tile_rows.reshape(1, capacity), tile_cols.reshape(1, capacity),
      features, cotangent, self_weight, neigh_weight, degrees.reshape(1, edge),
      adjacency.reshape(capacity, edge, edge))
    return pl.pallas_call(
        finish_kernel,
        out_shape=tuple(jax.ShapeDtypeStruct(x.shape, x.dtype) for x in results),
        in_specs=[vmem] * 4,
        out_specs=(vmem,) * 4,
        compiler_params=pltpu.CompilerParams(vmem_limit_bytes=60 * 2**20),
        name="write_outputs",
    )(*results)


def solution(mesh):
    in_specs = (
        P(("row", "col"), None),
        P(("row", "col"), None),
        P(),
        P(),
        P(("row", "col")),
        P("row", "col", None, None, None),
        P("row", "col", None),
        P("row", "col", None),
        P("row", "col"),
    )
    out_specs = (P(("row", "col"), None), P(("row", "col"), None), P(), P())
    n_row, n_col = mesh.shape["row"], mesh.shape["col"]
    return jax.shard_map(functools.partial(body, n_row, n_col), mesh=mesh,
                         in_specs=in_specs, out_specs=out_specs, check_vma=False)
```

```python
import functools

import jax
import jax.numpy as jnp
from jax import lax
from jax.experimental import pallas as pl
from jax.experimental.pallas import tpu as pltpu
from jax.sharding import PartitionSpec as P

MESH = pl.DeviceIdType.MESH
BF16 = jnp.bfloat16
F32 = jnp.float32
STEP = 4


def dot(a, b, contract=((1,), (0,))):
    return lax.dot_general(a, b, (contract, ((), ())), preferred_element_type=F32)


def each(low, high, step):
    if high - low <= 8:
        for index in range(low, high):
            step(index)
    else:
        def looped(index, carry):
            step(index)
            return carry
        lax.fori_loop(low, high, looped, 0)


def finish_kernel(*refs):
    count = len(refs) // 2
    for i in range(count):
        refs[count + i][...] = refs[i][...]


def layer_kernel(
    n_row, n_col,
    count_ref, rows_ref, cols_ref, feat_ref, cot_ref, self_ref, neigh_ref, deg_ref, tiles_hbm,
    hidden_ref, gfeat_ref, gself_ref, gneigh_ref,
    slot_lists, order_ref, bounds_ref, tiles, sums, dense, src, part_out, part_in, gm, back_out, back_in, w_out, w_in, q_out, q_in, fin, back_acc,
    lists_r, tiles_r, src_s, src_r, part_s, part_r, gm_s, gm_r, back_s, back_r,
    w_s, w_r, q_s, q_r, fin_s, fin_r,
):
    r = lax.axis_index("row")
    c = lax.axis_index("col")
    edge = feat_ref.shape[0]

    def row_at(m):
        other, bit = 0, 1
        while bit < n_row:
            other = other + bit * (((r // bit) + (m // bit)) % 2)
            bit *= 2
        return other

    def far_first(step):
        each(1, n_row, lambda d: step(n_row - d))

    def near_first(step):
        half = n_row // 2
        each(1, half, step)
        each(0, half, lambda d: step(n_row - 1 - d))

    def col_at(d):
        return lax.rem(c + d, n_col)

    def over_row(source, target, send, recv, d):
        return pltpu.make_async_remote_copy(
            src_ref=source, dst_ref=target, send_sem=send.at[d], recv_sem=recv.at[d],
            device_id=(row_at(d), c), device_id_type=MESH)

    def over_col(source, target, send, recv, d):
        return pltpu.make_async_remote_copy(
            src_ref=source, dst_ref=target, send_sem=send.at[d], recv_sem=recv.at[d],
            device_id=(r, col_at(d)), device_id_type=MESH)

    fetch = pltpu.make_async_copy(tiles_hbm, tiles, tiles_r)
    fetch.start()
    barrier = pltpu.get_barrier_semaphore()
    each(1, n_col, lambda d: pl.semaphore_signal(
        barrier, inc=1, device_id=(r, col_at(d)), device_id_type=MESH))
    each(1, n_row, lambda d: pl.semaphore_signal(
        barrier, inc=1, device_id=(row_at(d), c), device_id_type=MESH))

    capacity = tiles.shape[0]
    places = n_row * n_col
    slot_down = lax.broadcasted_iota(jnp.int32, (capacity, capacity), 0)
    slot_across = lax.broadcasted_iota(jnp.int32, (capacity, capacity), 1)
    key_row = jnp.where(slot_across[:1] < count_ref[...],
                        rows_ref[...] * n_col + cols_ref[...], places)
    key_col = jnp.sum(jnp.where(slot_down == slot_across, key_row, 0), axis=1, keepdims=True)
    ahead = (key_row < key_col) | ((key_row == key_col) & (slot_across < slot_down))
    rank = jnp.sum(jnp.where(ahead, 1, 0), axis=1, keepdims=True)
    slot_lists[0:1, :capacity] = jnp.sum(
        jnp.where(rank == slot_across, slot_down, 0), axis=0, keepdims=True)
    spots = lax.broadcasted_iota(jnp.int32, (capacity, slot_lists.shape[1]), 1)
    slot_lists[1:2, :] = jnp.sum(jnp.where(key_col < spots, 1, 0), axis=0, keepdims=True)
    lists = [pltpu.make_async_copy(slot_lists.at[pl.ds(i, 1)], ref, lists_r.at[i])
             for i, ref in enumerate((order_ref, bounds_ref))]
    for copy in lists:
        copy.start()
    pl.semaphore_wait(barrier, n_row + n_col - 2)

    def src_copy(d):
        return over_col(feat_ref, src.at[c], src_s, src_r, d)

    each(1, n_col, lambda d: src_copy(d).start())
    keep = pltpu.make_async_copy(feat_ref, src.at[c], src_r.at[0])
    keep.start()
    inv_row = lax.rsqrt(jnp.maximum(deg_ref[...], 1).astype(F32))
    down = lax.broadcasted_iota(jnp.int32, (edge, edge), 0)
    across = lax.broadcasted_iota(jnp.int32, (edge, edge), 1)
    inv_col = jnp.sum(jnp.where(down == across, inv_row, 0.0), axis=1, keepdims=True)
    own_linear = dot(feat_ref[...], self_ref[...])
    for copy in lists:
        copy.wait()
    fetch.wait()

    sums[0] = jnp.zeros(sums.shape[1:], BF16)

    def run(step, total):
        for k in range(STEP):
            slot = step * STEP + k
            total = total + tiles[order_ref[0, slot]].astype(F32).astype(BF16)
            sums[slot + 1] = total
        return total

    lax.fori_loop(0, capacity // STEP, run, jnp.zeros(sums.shape[1:], BF16))

    def place(row, carry):
        for col in range(n_col):
            spot = row * n_col + col
            rows = pl.ds(pl.multiple_of(row * edge, edge), edge)
            dense[rows, col * edge:(col + 1) * edge] = (
                sums[bounds_ref[0, spot + 1]] - sums[bounds_ref[0, spot]])
        return carry

    lax.fori_loop(0, n_row, place, 0)
    keep.wait()
    each(1, n_col, lambda d: src_copy(d).wait_recv())
    source = src[...].reshape(n_col * edge, src.shape[-1])

    def part_copy(d):
        return over_row(part_out.at[d], part_in.at[d], part_s, part_r, d)

    def partial(d):
        rows = pl.ds(pl.multiple_of(row_at(d) * edge, edge), edge)
        return dot(dense[rows, :], source)

    def send_part(d):
        part_out[d] = partial(d).astype(BF16)
        part_copy(d).start()

    far_first(send_part)
    agg = partial(0).astype(BF16).astype(F32)
    for d in range(1, n_row):
        part_copy(d).wait_recv()
        agg = agg + part_in[d].astype(F32)

    mixed = (agg * inv_col).astype(BF16)
    linear = own_linear + dot(mixed, neigh_ref[...])
    sigma = jax.nn.sigmoid(linear)
    slope = sigma * (1.0 + linear * (1.0 - sigma))
    grad_linear = (cot_ref[...].astype(F32) * slope).astype(BF16)
    gm[r] = (dot(neigh_ref[...], grad_linear, ((1,), (1,))) * inv_row).astype(BF16)

    def gm_copy(d):
        return over_row(gm.at[r], gm.at[r], gm_s, gm_r, d)

    far_first(lambda d: gm_copy(d).start())

    share = w_out.shape[1]
    both = jnp.concatenate([feat_ref[...], mixed], axis=1)
    w_out[...] = dot(both, grad_linear, ((0,), (0,))).reshape(w_out.shape)

    def w_copy(d):
        return over_col(w_out.at[col_at(d)], w_in.at[d], w_s, w_r, d)

    each(1, n_col, lambda d: w_copy(d).start())
    hidden_ref[...] = (linear * sigma).astype(BF16)
    own_grad = dot(grad_linear, self_ref[...], ((1,), (1,)))

    def q_copy(d):
        return over_row(q_out, q_in.at[d], q_s, q_r, d)

    def sum_over_col():
        total = w_out[c]
        for d in range(1, n_col):
            w_copy(d).wait_recv()
            total = total + w_in[d]
        q_out[...] = total.astype(BF16)
        far_first(lambda d: q_copy(d).start())
        return total

    def back_term(d):
        owner = row_at(d)
        rows = pl.ds(pl.multiple_of(owner * edge, edge), edge)
        return dot(gm[owner], dense[rows, :])

    def add_back(d):
        gm_copy(d).wait_recv()
        back_acc[...] += back_term(d)

    back_acc[...] = back_term(0)
    total = sum_over_col()
    near_first(add_back)

    for b in range(n_col):
        back_out[b] = back_acc[:, b * edge:(b + 1) * edge].astype(BF16)

    def back_copy(d):
        return over_col(back_out.at[col_at(d)], back_in.at[d], back_s, back_r, d)

    each(1, n_col, lambda d: back_copy(d).start())

    for d in range(1, n_row):
        q_copy(d).wait_recv()
        total = total + q_in[d].astype(F32)
    fin[c] = total.astype(BF16)

    def fin_copy(d):
        return over_col(fin.at[c], fin.at[c], fin_s, fin_r, d)

    each(1, n_col, lambda d: fin_copy(d).start())
    returned = back_out[c].astype(F32)
    for d in range(1, n_col):
        back_copy(d).wait_recv()
        returned = returned + back_in[d].astype(F32)
    gfeat_ref[...] = (own_grad + returned.T).astype(BF16)

    each(1, n_col, lambda d: fin_copy(d).wait_recv())
    grads = fin[...].reshape(n_col * share, fin.shape[-1]).astype(F32)
    half = gself_ref.shape[0]
    gself_ref[...] = grads[:half]
    gneigh_ref[...] = grads[half:]

    def drain_col(d):
        for copy in (src_copy, w_copy, back_copy, fin_copy):
            copy(d).wait_send()

    def drain_row(d):
        for copy in (part_copy, gm_copy, q_copy):
            copy(d).wait_send()

    each(1, n_col, drain_col)
    each(1, n_row, drain_row)


def body(n_row, n_col, features, cotangent, self_weight, neigh_weight, degrees,
         adjacency, tile_rows, tile_cols, tile_count):
    edge = adjacency.shape[-1]
    capacity = adjacency.shape[2]
    hidden_units = features.shape[-1]
    rows, cols = n_row * edge, n_col * edge
    vmem = pl.BlockSpec(memory_space=pltpu.VMEM)
    hbm = pl.BlockSpec(memory_space=pltpu.HBM)
    list_width = -(-(n_row * n_col + 1) // 128) * 128
    share = 2 * hidden_units // n_col
    block = (edge, hidden_units)
    dma = pltpu.SemaphoreType.DMA
    results = pl.pallas_call(
        functools.partial(layer_kernel, n_row, n_col),
        out_shape=(
            jax.ShapeDtypeStruct(block, BF16),
            jax.ShapeDtypeStruct(block, BF16),
            jax.ShapeDtypeStruct(self_weight.shape, F32),
            jax.ShapeDtypeStruct(neigh_weight.shape, F32),
        ),
        in_specs=[vmem] * 8 + [hbm],
        out_specs=(vmem,) * 4,
        scratch_shapes=[
            pltpu.VMEM((8, list_width), jnp.int32),
            pltpu.SMEM((1, list_width), jnp.int32),
            pltpu.SMEM((1, list_width), jnp.int32),
            pltpu.VMEM((capacity, edge, edge), jnp.int32),
            pltpu.VMEM((capacity + 1, edge, edge), BF16),
            pltpu.VMEM((rows, cols), BF16),
            pltpu.VMEM((n_col,) + block, BF16),
            pltpu.VMEM((n_row,) + block, BF16),
            pltpu.VMEM((n_row,) + block, BF16),
            pltpu.VMEM((n_row,) + block, BF16),
            pltpu.VMEM((n_col,) + block, BF16),
            pltpu.VMEM((n_col,) + block, BF16),
            pltpu.VMEM((n_col, share, hidden_units), F32),
            pltpu.VMEM((n_col, share, hidden_units), F32),
            pltpu.VMEM((share, hidden_units), BF16),
            pltpu.VMEM((n_row, share, hidden_units), BF16),
            pltpu.VMEM((n_col, share, hidden_units), BF16),
            pltpu.VMEM((hidden_units, cols), F32),
            dma((2,)),
            dma,
            dma((n_col,)), dma((n_col,)),
            dma((n_row,)), dma((n_row,)),
            dma((n_row,)), dma((n_row,)),
            dma((n_col,)), dma((n_col,)),
            dma((n_col,)), dma((n_col,)),
            dma((n_row,)), dma((n_row,)),
            dma((n_col,)), dma((n_col,)),
        ],
        compiler_params=pltpu.CompilerParams(
            collective_id=0, has_side_effects=True, vmem_limit_bytes=58 * 2**20),
        name="layer_exchange",
    )(tile_count.reshape(1, 1), tile_rows.reshape(1, capacity), tile_cols.reshape(1, capacity),
      features, cotangent, self_weight, neigh_weight, degrees.reshape(1, edge),
      adjacency.reshape(capacity, edge, edge))
    return pl.pallas_call(
        finish_kernel,
        out_shape=tuple(jax.ShapeDtypeStruct(x.shape, x.dtype) for x in results),
        in_specs=[vmem] * 4,
        out_specs=(vmem,) * 4,
        compiler_params=pltpu.CompilerParams(vmem_limit_bytes=60 * 2**20),
        name="write_outputs",
    )(*results)


def solution(mesh):
    in_specs = (
        P(("row", "col"), None),
        P(("row", "col"), None),
        P(),
        P(),
        P(("row", "col")),
        P("row", "col", None, None, None),
        P("row", "col", None),
        P("row", "col", None),
        P("row", "col"),
    )
    out_specs = (P(("row", "col"), None), P(("row", "col"), None), P(), P())
    n_row, n_col = mesh.shape["row"], mesh.shape["col"]
    return jax.shard_map(functools.partial(body, n_row, n_col), mesh=mesh,
                         in_specs=in_specs, out_specs=out_specs, check_vma=False)
```

```python
import functools

import jax
import jax.numpy as jnp
from jax import lax
from jax.experimental import pallas as pl
from jax.experimental.pallas import tpu as pltpu
from jax.sharding import PartitionSpec as P

MESH = pl.DeviceIdType.MESH
BF16 = jnp.bfloat16
F32 = jnp.float32
STEP = 4


def dot(a, b, contract=((1,), (0,))):
    return lax.dot_general(a, b, (contract, ((), ())), preferred_element_type=F32)


def each(low, high, step):
    if high - low <= 8:
        for index in range(low, high):
            step(index)
    else:
        def looped(index, carry):
            step(index)
            return carry
        lax.fori_loop(low, high, looped, 0)


def finish_kernel(*refs):
    count = len(refs) // 2
    for i in range(count):
        refs[count + i][...] = refs[i][...]


def layer_kernel(
    n_row, n_col,
    count_ref, rows_ref, cols_ref, feat_ref, cot_ref, self_ref, neigh_ref, deg_ref, tiles_hbm,
    hidden_ref, gfeat_ref, gself_ref, gneigh_ref,
    slot_lists, order_ref, bounds_ref, tiles, sums, dense, src, part_out, part_in, gm, back_out, back_in, w_out, w_in, q_out, q_in, fin, back_acc,
    lists_r, tiles_r, src_s, src_r, part_s, part_r, gm_s, gm_r, back_s, back_r,
    w_s, w_r, q_s, q_r, fin_s, fin_r,
):
    r = lax.axis_index("row")
    c = lax.axis_index("col")
    edge = feat_ref.shape[0]

    n_line = n_row // 2
    line, side = r // 2, lax.rem(r, 2)

    def row_at(d):
        return lax.rem(line + d // 2, n_line) * 2 + lax.rem(side + d % 2, 2)

    def col_at(d):
        return lax.rem(c + d, n_col)

    def over_row(source, target, send, recv, d):
        return pltpu.make_async_remote_copy(
            src_ref=source, dst_ref=target, send_sem=send.at[d], recv_sem=recv.at[d],
            device_id=(row_at(d), c), device_id_type=MESH)

    def over_col(source, target, send, recv, d):
        return pltpu.make_async_remote_copy(
            src_ref=source, dst_ref=target, send_sem=send.at[d], recv_sem=recv.at[d],
            device_id=(r, col_at(d)), device_id_type=MESH)

    fetch = pltpu.make_async_copy(tiles_hbm, tiles, tiles_r)
    fetch.start()
    barrier = pltpu.get_barrier_semaphore()
    each(1, n_col, lambda d: pl.semaphore_signal(
        barrier, inc=1, device_id=(r, col_at(d)), device_id_type=MESH))
    each(1, n_row, lambda d: pl.semaphore_signal(
        barrier, inc=1, device_id=(row_at(d), c), device_id_type=MESH))

    capacity = tiles.shape[0]
    places = n_row * n_col
    slot_down = lax.broadcasted_iota(jnp.int32, (capacity, capacity), 0)
    slot_across = lax.broadcasted_iota(jnp.int32, (capacity, capacity), 1)
    key_row = jnp.where(slot_across[:1] < count_ref[...],
                        rows_ref[...] * n_col + cols_ref[...], places)
    key_col = jnp.sum(jnp.where(slot_down == slot_across, key_row, 0), axis=1, keepdims=True)
    ahead = (key_row < key_col) | ((key_row == key_col) & (slot_across < slot_down))
    rank = jnp.sum(jnp.where(ahead, 1, 0), axis=1, keepdims=True)
    slot_lists[0:1, :capacity] = jnp.sum(
        jnp.where(rank == slot_across, slot_down, 0), axis=0, keepdims=True)
    spots = lax.broadcasted_iota(jnp.int32, (capacity, slot_lists.shape[1]), 1)
    slot_lists[1:2, :] = jnp.sum(jnp.where(key_col < spots, 1, 0), axis=0, keepdims=True)
    lists = [pltpu.make_async_copy(slot_lists.at[pl.ds(i, 1)], ref, lists_r.at[i])
             for i, ref in enumerate((order_ref, bounds_ref))]
    for copy in lists:
        copy.start()
    pl.semaphore_wait(barrier, n_row + n_col - 2)

    def src_copy(d):
        return over_col(feat_ref, src.at[c], src_s, src_r, d)

    each(1, n_col, lambda d: src_copy(d).start())
    keep = pltpu.make_async_copy(feat_ref, src.at[c], src_r.at[0])
    keep.start()
    inv_row = lax.rsqrt(jnp.maximum(deg_ref[...], 1).astype(F32))
    down = lax.broadcasted_iota(jnp.int32, (edge, edge), 0)
    across = lax.broadcasted_iota(jnp.int32, (edge, edge), 1)
    inv_col = jnp.sum(jnp.where(down == across, inv_row, 0.0), axis=1, keepdims=True)
    own_linear = dot(feat_ref[...], self_ref[...])
    for copy in lists:
        copy.wait()
    fetch.wait()

    sums[0] = jnp.zeros(sums.shape[1:], BF16)

    def run(step, total):
        for k in range(STEP):
            slot = step * STEP + k
            total = total + tiles[order_ref[0, slot]].astype(F32).astype(BF16)
            sums[slot + 1] = total
        return total

    lax.fori_loop(0, capacity // STEP, run, jnp.zeros(sums.shape[1:], BF16))

    def place(row, carry):
        for col in range(n_col):
            spot = row * n_col + col
            rows = pl.ds(pl.multiple_of(row * edge, edge), edge)
            dense[rows, col * edge:(col + 1) * edge] = (
                sums[bounds_ref[0, spot + 1]] - sums[bounds_ref[0, spot]])
        return carry

    lax.fori_loop(0, n_row, place, 0)
    keep.wait()
    each(1, n_col, lambda d: src_copy(d).wait_recv())
    source = src[...].reshape(n_col * edge, src.shape[-1])

    def part_copy(d):
        leaving = part_out.at[d // 2 * 2 + lax.rem(side + d % 2, 2)]
        return over_row(leaving, part_in.at[d], part_s, part_r, d)

    def partial(e):
        first = lax.rem(line + e, n_line) * 2
        rows = pl.ds(pl.multiple_of(first * edge, 2 * edge), 2 * edge)
        pair = dot(dense[rows, :], source).astype(BF16)
        part_out[pl.ds(2 * e, 2)] = pair.reshape((2,) + part_out.shape[1:])

    def send_part(e):
        partial(e)
        part_copy(2 * e).start()
        part_copy(2 * e + 1).start()

    each(1, n_line, send_part)
    partial(0)
    part_copy(1).start()
    agg = part_out[side].astype(F32)
    for d in range(1, n_row):
        part_copy(d).wait_recv()
        agg = agg + part_in[d].astype(F32)

    mixed = (agg * inv_col).astype(BF16)
    linear = own_linear + dot(mixed, neigh_ref[...])
    sigma = jax.nn.sigmoid(linear)
    slope = sigma * (1.0 + linear * (1.0 - sigma))
    grad_linear = (cot_ref[...].astype(F32) * slope).astype(BF16)
    share = w_out.shape[1]
    both = jnp.concatenate([feat_ref[...], mixed], axis=1)
    w_out[...] = dot(both, grad_linear, ((0,), (0,))).reshape(w_out.shape)

    def w_copy(d):
        return over_col(w_out.at[col_at(d)], w_in.at[d], w_s, w_r, d)

    each(1, n_col, lambda d: w_copy(d).start())
    gm[r] = (dot(neigh_ref[...], grad_linear, ((1,), (1,))) * inv_row).astype(BF16)

    def gm_copy(d):
        return over_row(gm.at[r], gm.at[r], gm_s, gm_r, d)

    each(1, n_row, lambda d: gm_copy(d).start())
    hidden_ref[...] = (linear * sigma).astype(BF16)
    own_grad = dot(grad_linear, self_ref[...], ((1,), (1,)))

    def q_copy(d):
        return over_row(q_out, q_in.at[d], q_s, q_r, d)

    def sum_over_col():
        total = w_out[c]
        for d in range(1, n_col):
            w_copy(d).wait_recv()
            total = total + w_in[d]
        q_out[...] = total.astype(BF16)
        each(1, n_row, lambda d: q_copy(d).start())
        return total

    def back_term(e):
        first = lax.rem(line - e + n_line, n_line) * 2
        rows = pl.ds(pl.multiple_of(first * edge, 2 * edge), 2 * edge)
        return dot(jnp.concatenate([gm[first], gm[first + 1]], axis=1), dense[rows, :])

    def add_back(e):
        gm_copy(2 * e).wait_recv()
        gm_copy(2 * e + 1).wait_recv()
        back_acc[...] += back_term(e)

    total = sum_over_col()
    gm_copy(1).wait_recv()
    back_acc[...] = back_term(0)
    each(1, n_line, add_back)

    for b in range(n_col):
        back_out[b] = back_acc[:, b * edge:(b + 1) * edge].astype(BF16)

    def back_copy(d):
        return over_col(back_out.at[col_at(d)], back_in.at[d], back_s, back_r, d)

    each(1, n_col, lambda d: back_copy(d).start())

    for d in range(1, n_row):
        q_copy(d).wait_recv()
        total = total + q_in[d].astype(F32)
    fin[c] = total.astype(BF16)

    def fin_copy(d):
        return over_col(fin.at[c], fin.at[c], fin_s, fin_r, d)

    each(1, n_col, lambda d: fin_copy(d).start())
    returned = back_out[c].astype(F32)
    for d in range(1, n_col):
        back_copy(d).wait_recv()
        returned = returned + back_in[d].astype(F32)
    gfeat_ref[...] = (own_grad + returned.T).astype(BF16)

    each(1, n_col, lambda d: fin_copy(d).wait_recv())
    grads = fin[...].reshape(n_col * share, fin.shape[-1]).astype(F32)
    half = gself_ref.shape[0]
    gself_ref[...] = grads[:half]
    gneigh_ref[...] = grads[half:]

    def drain_col(d):
        for copy in (src_copy, w_copy, back_copy, fin_copy):
            copy(d).wait_send()

    def drain_row(d):
        for copy in (part_copy, gm_copy, q_copy):
            copy(d).wait_send()

    each(1, n_col, drain_col)
    each(1, n_row, drain_row)


def body(n_row, n_col, features, cotangent, self_weight, neigh_weight, degrees,
         adjacency, tile_rows, tile_cols, tile_count):
    edge = adjacency.shape[-1]
    capacity = adjacency.shape[2]
    hidden_units = features.shape[-1]
    rows, cols = n_row * edge, n_col * edge
    vmem = pl.BlockSpec(memory_space=pltpu.VMEM)
    hbm = pl.BlockSpec(memory_space=pltpu.HBM)
    list_width = -(-(n_row * n_col + 1) // 128) * 128
    share = 2 * hidden_units // n_col
    block = (edge, hidden_units)
    dma = pltpu.SemaphoreType.DMA
    results = pl.pallas_call(
        functools.partial(layer_kernel, n_row, n_col),
        out_shape=(
            jax.ShapeDtypeStruct(block, BF16),
            jax.ShapeDtypeStruct(block, BF16),
            jax.ShapeDtypeStruct(self_weight.shape, F32),
            jax.ShapeDtypeStruct(neigh_weight.shape, F32),
        ),
        in_specs=[vmem] * 8 + [hbm],
        out_specs=(vmem,) * 4,
        scratch_shapes=[
            pltpu.VMEM((8, list_width), jnp.int32),
            pltpu.SMEM((1, list_width), jnp.int32),
            pltpu.SMEM((1, list_width), jnp.int32),
            pltpu.VMEM((capacity, edge, edge), jnp.int32),
            pltpu.VMEM((capacity + 1, edge, edge), BF16),
            pltpu.VMEM((rows, cols), BF16),
            pltpu.VMEM((n_col,) + block, BF16),
            pltpu.VMEM((n_row,) + block, BF16),
            pltpu.VMEM((n_row,) + block, BF16),
            pltpu.VMEM((n_row,) + block, BF16),
            pltpu.VMEM((n_col,) + block, BF16),
            pltpu.VMEM((n_col,) + block, BF16),
            pltpu.VMEM((n_col, share, hidden_units), F32),
            pltpu.VMEM((n_col, share, hidden_units), F32),
            pltpu.VMEM((share, hidden_units), BF16),
            pltpu.VMEM((n_row, share, hidden_units), BF16),
            pltpu.VMEM((n_col, share, hidden_units), BF16),
            pltpu.VMEM((hidden_units, cols), F32),
            dma((2,)),
            dma,
            dma((n_col,)), dma((n_col,)),
            dma((n_row,)), dma((n_row,)),
            dma((n_row,)), dma((n_row,)),
            dma((n_col,)), dma((n_col,)),
            dma((n_col,)), dma((n_col,)),
            dma((n_row,)), dma((n_row,)),
            dma((n_col,)), dma((n_col,)),
        ],
        compiler_params=pltpu.CompilerParams(
            collective_id=0, has_side_effects=True, vmem_limit_bytes=58 * 2**20),
        name="layer_exchange",
    )(tile_count.reshape(1, 1), tile_rows.reshape(1, capacity), tile_cols.reshape(1, capacity),
      features, cotangent, self_weight, neigh_weight, degrees.reshape(1, edge),
      adjacency.reshape(capacity, edge, edge))
    return pl.pallas_call(
        finish_kernel,
        out_shape=tuple(jax.ShapeDtypeStruct(x.shape, x.dtype) for x in results),
        in_specs=[vmem] * 4,
        out_specs=(vmem,) * 4,
        compiler_params=pltpu.CompilerParams(vmem_limit_bytes=60 * 2**20),
        name="write_outputs",
    )(*results)


def solution(mesh):
    in_specs = (
        P(("row", "col"), None),
        P(("row", "col"), None),
        P(),
        P(),
        P(("row", "col")),
        P("row", "col", None, None, None),
        P("row", "col", None),
        P("row", "col", None),
        P("row", "col"),
    )
    out_specs = (P(("row", "col"), None), P(("row", "col"), None), P(), P())
    n_row, n_col = mesh.shape["row"], mesh.shape["col"]
    return jax.shard_map(functools.partial(body, n_row, n_col), mesh=mesh,
                         in_specs=in_specs, out_specs=out_specs, check_vma=False)
```

```python
import functools

import jax
import jax.numpy as jnp
from jax import lax
from jax.experimental import pallas as pl
from jax.experimental.pallas import tpu as pltpu
from jax.sharding import PartitionSpec as P

MESH = pl.DeviceIdType.MESH
BF16 = jnp.bfloat16
F32 = jnp.float32
STEP = 4


def dot(a, b, contract=((1,), (0,))):
    return lax.dot_general(a, b, (contract, ((), ())), preferred_element_type=F32)


def each(low, high, step):
    if high - low <= 8:
        for index in range(low, high):
            step(index)
    else:
        def looped(index, carry):
            step(index)
            return carry
        lax.fori_loop(low, high, looped, 0)


def finish_kernel(*refs):
    count = len(refs) // 2
    for i in range(count):
        refs[count + i][...] = refs[i][...]


def layer_kernel(
    n_row, n_col,
    count_ref, rows_ref, cols_ref, feat_ref, cot_ref, self_ref, neigh_ref, deg_ref, tiles_hbm,
    hidden_ref, gfeat_ref, gself_ref, gneigh_ref,
    slot_lists, order_ref, bounds_ref, tiles, sums, dense, src, part_out, part_in, gm, back_out, back_in, w_out, w_in, q_out, q_in, fin, back_acc,
    lists_r, tiles_r, src_s, src_r, part_s, part_r, gm_s, gm_r, back_s, back_r,
    w_s, w_r, q_s, q_r, fin_s, fin_r,
):
    r = lax.axis_index("row")
    c = lax.axis_index("col")
    edge = feat_ref.shape[0]

    n_line = n_row // 2
    line, side = r // 2, lax.rem(r, 2)

    def row_at(d):
        return lax.rem(line + d // 2, n_line) * 2 + lax.rem(side + d % 2, 2)

    def col_at(d):
        return lax.rem(c + d, n_col)

    def over_row(source, target, send, recv, d):
        return pltpu.make_async_remote_copy(
            src_ref=source, dst_ref=target, send_sem=send.at[d], recv_sem=recv.at[d],
            device_id=(row_at(d), c), device_id_type=MESH)

    def over_col(source, target, send, recv, d):
        return pltpu.make_async_remote_copy(
            src_ref=source, dst_ref=target, send_sem=send.at[d], recv_sem=recv.at[d],
            device_id=(r, col_at(d)), device_id_type=MESH)

    fetch = pltpu.make_async_copy(tiles_hbm, tiles, tiles_r)
    fetch.start()
    barrier = pltpu.get_barrier_semaphore()
    each(1, n_col, lambda d: pl.semaphore_signal(
        barrier, inc=1, device_id=(r, col_at(d)), device_id_type=MESH))
    each(1, n_row, lambda d: pl.semaphore_signal(
        barrier, inc=1, device_id=(row_at(d), c), device_id_type=MESH))

    capacity = tiles.shape[0]
    places = n_row * n_col
    slot_down = lax.broadcasted_iota(jnp.int32, (capacity, capacity), 0)
    slot_across = lax.broadcasted_iota(jnp.int32, (capacity, capacity), 1)
    key_row = jnp.where(slot_across[:1] < count_ref[...],
                        rows_ref[...] * n_col + cols_ref[...], places)
    key_col = jnp.sum(jnp.where(slot_down == slot_across, key_row, 0), axis=1, keepdims=True)
    ahead = (key_row < key_col) | ((key_row == key_col) & (slot_across < slot_down))
    rank = jnp.sum(jnp.where(ahead, 1, 0), axis=1, keepdims=True)
    slot_lists[0:1, :capacity] = jnp.sum(
        jnp.where(rank == slot_across, slot_down, 0), axis=0, keepdims=True)
    spots = lax.broadcasted_iota(jnp.int32, (capacity, slot_lists.shape[1]), 1)
    slot_lists[1:2, :] = jnp.sum(jnp.where(key_col < spots, 1, 0), axis=0, keepdims=True)
    lists = [pltpu.make_async_copy(slot_lists.at[pl.ds(i, 1)], ref, lists_r.at[i])
             for i, ref in enumerate((order_ref, bounds_ref))]
    for copy in lists:
        copy.start()
    for copy in lists:
        copy.wait()
    fetch.wait()

    sums[0] = jnp.zeros(sums.shape[1:], BF16)

    def run(step, total):
        for k in range(STEP):
            slot = step * STEP + k
            total = total + tiles[order_ref[0, slot]].astype(F32).astype(BF16)
            sums[slot + 1] = total
        return total

    lax.fori_loop(0, capacity // STEP, run, jnp.zeros(sums.shape[1:], BF16))
    pl.semaphore_wait(barrier, n_row + n_col - 2)

    def src_copy(d):
        return over_col(feat_ref, src.at[c], src_s, src_r, d)

    each(1, n_col, lambda d: src_copy(d).start())
    keep = pltpu.make_async_copy(feat_ref, src.at[c], src_r.at[0])
    keep.start()
    inv_row = lax.rsqrt(jnp.maximum(deg_ref[...], 1).astype(F32))
    down = lax.broadcasted_iota(jnp.int32, (edge, edge), 0)
    across = lax.broadcasted_iota(jnp.int32, (edge, edge), 1)
    inv_col = jnp.sum(jnp.where(down == across, inv_row, 0.0), axis=1, keepdims=True)
    own_linear = dot(feat_ref[...], self_ref[...])
    def place(row, carry):
        for col in range(n_col):
            spot = row * n_col + col
            rows = pl.ds(pl.multiple_of(row * edge, edge), edge)
            dense[rows, col * edge:(col + 1) * edge] = (
                sums[bounds_ref[0, spot + 1]] - sums[bounds_ref[0, spot]])
        return carry

    lax.fori_loop(0, n_row, place, 0)
    keep.wait()
    each(1, n_col, lambda d: src_copy(d).wait_recv())
    source = src[...].reshape(n_col * edge, src.shape[-1])

    def part_copy(d):
        leaving = part_out.at[d // 2 * 2 + lax.rem(side + d % 2, 2)]
        return over_row(leaving, part_in.at[d], part_s, part_r, d)

    def partial(e):
        first = lax.rem(line + e, n_line) * 2
        rows = pl.ds(pl.multiple_of(first * edge, 2 * edge), 2 * edge)
        pair = dot(dense[rows, :], source).astype(BF16)
        part_out[pl.ds(2 * e, 2)] = pair.reshape((2,) + part_out.shape[1:])

    def send_part(e):
        partial(e)
        part_copy(2 * e).start()
        part_copy(2 * e + 1).start()

    each(1, n_line, send_part)
    partial(0)
    part_copy(1).start()
    agg = part_out[side].astype(F32)
    for d in range(1, n_row):
        part_copy(d).wait_recv()
        agg = agg + part_in[d].astype(F32)

    mixed = (agg * inv_col).astype(BF16)
    linear = own_linear + dot(mixed, neigh_ref[...])
    sigma = jax.nn.sigmoid(linear)
    slope = sigma * (1.0 + linear * (1.0 - sigma))
    grad_linear = (cot_ref[...].astype(F32) * slope).astype(BF16)
    share = w_out.shape[1]
    both = jnp.concatenate([feat_ref[...], mixed], axis=1)
    w_out[...] = dot(both, grad_linear, ((0,), (0,))).reshape(w_out.shape)

    def w_copy(d):
        return over_col(w_out.at[col_at(d)], w_in.at[d], w_s, w_r, d)

    each(1, n_col, lambda d: w_copy(d).start())
    gm[r] = (dot(neigh_ref[...], grad_linear, ((1,), (1,))) * inv_row).astype(BF16)

    def gm_copy(d):
        return over_row(gm.at[r], gm.at[r], gm_s, gm_r, d)

    each(1, n_row, lambda d: gm_copy(d).start())
    hidden_ref[...] = (linear * sigma).astype(BF16)
    own_grad = dot(grad_linear, self_ref[...], ((1,), (1,)))

    def q_copy(d):
        return over_row(q_out, q_in.at[d], q_s, q_r, d)

    def sum_over_col():
        total = w_out[c]
        for d in range(1, n_col):
            w_copy(d).wait_recv()
            total = total + w_in[d]
        q_out[...] = total.astype(BF16)
        each(1, n_row, lambda d: q_copy(d).start())
        return total

    def back_term(e):
        first = lax.rem(line - e + n_line, n_line) * 2
        rows = pl.ds(pl.multiple_of(first * edge, 2 * edge), 2 * edge)
        return dot(jnp.concatenate([gm[first], gm[first + 1]], axis=1), dense[rows, :])

    def add_back(e):
        gm_copy(2 * e).wait_recv()
        gm_copy(2 * e + 1).wait_recv()
        back_acc[...] += back_term(e)

    total = sum_over_col()
    gm_copy(1).wait_recv()
    back_acc[...] = back_term(0)
    each(1, n_line, add_back)

    for b in range(n_col):
        back_out[b] = back_acc[:, b * edge:(b + 1) * edge].astype(BF16)

    def back_copy(d):
        return over_col(back_out.at[col_at(d)], back_in.at[d], back_s, back_r, d)

    each(1, n_col, lambda d: back_copy(d).start())

    for d in range(1, n_row):
        q_copy(d).wait_recv()
        total = total + q_in[d].astype(F32)
    fin[c] = total.astype(BF16)

    def fin_copy(d):
        return over_col(fin.at[c], fin.at[c], fin_s, fin_r, d)

    each(1, n_col, lambda d: fin_copy(d).start())
    returned = back_out[c].astype(F32)
    for d in range(1, n_col):
        back_copy(d).wait_recv()
        returned = returned + back_in[d].astype(F32)
    gfeat_ref[...] = (own_grad + returned.T).astype(BF16)

    each(1, n_col, lambda d: fin_copy(d).wait_recv())
    grads = fin[...].reshape(n_col * share, fin.shape[-1]).astype(F32)
    half = gself_ref.shape[0]
    gself_ref[...] = grads[:half]
    gneigh_ref[...] = grads[half:]

    def drain_col(d):
        for copy in (src_copy, w_copy, back_copy, fin_copy):
            copy(d).wait_send()

    def drain_row(d):
        for copy in (part_copy, gm_copy, q_copy):
            copy(d).wait_send()

    each(1, n_col, drain_col)
    each(1, n_row, drain_row)


def body(n_row, n_col, features, cotangent, self_weight, neigh_weight, degrees,
         adjacency, tile_rows, tile_cols, tile_count):
    edge = adjacency.shape[-1]
    capacity = adjacency.shape[2]
    hidden_units = features.shape[-1]
    rows, cols = n_row * edge, n_col * edge
    vmem = pl.BlockSpec(memory_space=pltpu.VMEM)
    hbm = pl.BlockSpec(memory_space=pltpu.HBM)
    list_width = -(-(n_row * n_col + 1) // 128) * 128
    share = 2 * hidden_units // n_col
    block = (edge, hidden_units)
    dma = pltpu.SemaphoreType.DMA
    results = pl.pallas_call(
        functools.partial(layer_kernel, n_row, n_col),
        out_shape=(
            jax.ShapeDtypeStruct(block, BF16),
            jax.ShapeDtypeStruct(block, BF16),
            jax.ShapeDtypeStruct(self_weight.shape, F32),
            jax.ShapeDtypeStruct(neigh_weight.shape, F32),
        ),
        in_specs=[vmem] * 8 + [hbm],
        out_specs=(vmem,) * 4,
        scratch_shapes=[
            pltpu.VMEM((8, list_width), jnp.int32),
            pltpu.SMEM((1, list_width), jnp.int32),
            pltpu.SMEM((1, list_width), jnp.int32),
            pltpu.VMEM((capacity, edge, edge), jnp.int32),
            pltpu.VMEM((capacity + 1, edge, edge), BF16),
            pltpu.VMEM((rows, cols), BF16),
            pltpu.VMEM((n_col,) + block, BF16),
            pltpu.VMEM((n_row,) + block, BF16),
            pltpu.VMEM((n_row,) + block, BF16),
            pltpu.VMEM((n_row,) + block, BF16),
            pltpu.VMEM((n_col,) + block, BF16),
            pltpu.VMEM((n_col,) + block, BF16),
            pltpu.VMEM((n_col, share, hidden_units), F32),
            pltpu.VMEM((n_col, share, hidden_units), F32),
            pltpu.VMEM((share, hidden_units), BF16),
            pltpu.VMEM((n_row, share, hidden_units), BF16),
            pltpu.VMEM((n_col, share, hidden_units), BF16),
            pltpu.VMEM((hidden_units, cols), F32),
            dma((2,)),
            dma,
            dma((n_col,)), dma((n_col,)),
            dma((n_row,)), dma((n_row,)),
            dma((n_row,)), dma((n_row,)),
            dma((n_col,)), dma((n_col,)),
            dma((n_col,)), dma((n_col,)),
            dma((n_row,)), dma((n_row,)),
            dma((n_col,)), dma((n_col,)),
        ],
        compiler_params=pltpu.CompilerParams(
            collective_id=0, has_side_effects=True, vmem_limit_bytes=58 * 2**20),
        name="layer_exchange",
    )(tile_count.reshape(1, 1), tile_rows.reshape(1, capacity), tile_cols.reshape(1, capacity),
      features, cotangent, self_weight, neigh_weight, degrees.reshape(1, edge),
      adjacency.reshape(capacity, edge, edge))
    return pl.pallas_call(
        finish_kernel,
        out_shape=tuple(jax.ShapeDtypeStruct(x.shape, x.dtype) for x in results),
        in_specs=[vmem] * 4,
        out_specs=(vmem,) * 4,
        compiler_params=pltpu.CompilerParams(vmem_limit_bytes=60 * 2**20),
        name="write_outputs",
    )(*results)


def solution(mesh):
    in_specs = (
        P(("row", "col"), None),
        P(("row", "col"), None),
        P(),
        P(),
        P(("row", "col")),
        P("row", "col", None, None, None),
        P("row", "col", None),
        P("row", "col", None),
        P("row", "col"),
    )
    out_specs = (P(("row", "col"), None), P(("row", "col"), None), P(), P())
    n_row, n_col = mesh.shape["row"], mesh.shape["col"]
    return jax.shard_map(functools.partial(body, n_row, n_col), mesh=mesh,
                         in_specs=in_specs, out_specs=out_specs, check_vma=False)
```
